32 devices in a mesh: tok: 8 (over y, x, core), hid: 4 (over z).
Axes of the slice: x: 2, y: 2, z: 4, core: 2. Of those that a mesh axis runs over, the one named last changes fastest.
Arguments:
- tokens: bfloat16 [6144, 2048], P('tok', 'hid')
- qkv_weight: bfloat16 [2048, 6144], P('tok', 'hid')
- out_weight: bfloat16 [2048, 2048], P('tok', 'hid'), may hold values from -0.125 to 0.125
- neighbours: int32 [96, 9], replicated, may hold values from 0 to 95, as said below
- counts: int32 [96], replicated, may hold values from 7 to 9
Outputs:
- attended: bfloat16 [6144, 2048], P('tok', 'hid')
The draws below stay inside these ranges and needn't reach their ends.
Inputs may be any that keep to these rules, and one draw needn't show every extreme that they name: `neighbours`: entry 0 of each list is the block itself. Block b lies on index b // 12 of tok. Among the valid entries of the lists of one device's blocks, at most 2 distinct blocks of any one other device are named, and every device names exactly 2 blocks of some other device.
All inputs are finite; a program needn't handle non-finite values.
Results may differ from the reference program's by a relative error of at most 0.012.
Values may be sent and summed in bfloat16 or wider, within the bound.
No kernel may reach another device: no remote copies, remote signals or barrier semaphores. Data moves between devices by JAX's collectives and lax.ppermute only.
A program may use at most 128 MiB of HBM per device.

```python
import jax
import jax.numpy as jnp
from jax import lax

D = 2048
HEADS = 16
HEAD_WIDTH = 128
BLK = 64
NEIGH = 9
SLOTS = 2
BLK_DEV = 12
NBLK = 96
TOKENS = 6144


def draw_tokens(key, part):
    first = jax.random.fold_in(key, 0)
    base = jax.random.normal(first, (TOKENS, D), jnp.float32)
    return base.astype(jnp.bfloat16)


def draw_qkv_weight(key, part):
    first = jax.random.fold_in(key, 0)
    base = jax.random.normal(first, (D, HEADS, 3, HEAD_WIDTH), jnp.float32)
    factors = jnp.array([2.0, 2.0, 1.0], jnp.float32)[None, None, :, None] * D ** (-0.5)
    return (base * factors).reshape(D, 3 * D).astype(jnp.bfloat16)


def draw_neighbours(key, part):
    devices = NBLK // BLK_DEV
    first, second, third = jax.random.split(key, 3)
    block_offsets = jax.random.randint(first, (devices, devices), 0, BLK_DEV - SLOTS + 1)
    peers = jax.random.randint(second, (NBLK, NEIGH), 0, devices)
    offsets = jax.random.randint(third, (NBLK, NEIGH), 0, SLOTS)
    blocks = jnp.arange(NBLK).astype(jnp.int32)
    homes = blocks // BLK_DEV
    locals_index = blocks % BLK_DEV
    forced = locals_index < SLOTS
    peers = peers.at[:, 1].set(jnp.where(forced, (homes + 1) % devices, peers[:, 1]))
    offsets = offsets.at[:, 1].set(jnp.where(forced, locals_index, offsets[:, 1]))
    picked = peers * BLK_DEV + block_offsets[homes[:, None], peers] + offsets
    picked = picked.at[:, 0].set(blocks)
    return picked.astype(jnp.int32)


def place_ends(values, own_key, least, top_value):
    spot = [jax.random.randint(jax.random.fold_in(own_key, axis), (), 0, length) for axis, length in enumerate(values.shape)]
    widest = values.shape.index(max(values.shape))
    beside = spot[:widest] + [(spot[widest] + 1) % values.shape[widest]] + spot[widest + 1:]
    return values.at[tuple(spot)].set(least).at[tuple(beside)].set(top_value)


def level_of(own_key, shape, cuts, low, top_value):
    loudness, own = 1.0, jax.random.fold_in(own_key, 6)
    for axis_at, parts in cuts:
        draws = jnp.exp(jax.random.uniform(jax.random.fold_in(own, axis_at), (parts,), jnp.float32, low / len(cuts), top_value / len(cuts)))
        loudness = loudness * jnp.repeat(draws, shape[axis_at] // parts).reshape([-1 if axis == axis_at else 1 for axis in range(len(shape))])
    return loudness


def scatter_about(own_key, shape, spread, reach, cuts=(), kind=jnp.bfloat16):
    values = spread * jax.random.normal(own_key, shape, jnp.float32)
    if cuts:
        values = values * level_of(own_key, shape, cuts, -0.22, 0.18)
    return jnp.clip(values, -reach, reach).astype(kind)


def setup_inputs(seed: int = 0) -> dict:
    key_list = jax.random.split(jax.random.key(seed), 6)
    return {
        "tokens": draw_tokens(jax.random.fold_in(key_list[5], 71), 0),
        "qkv_weight": draw_qkv_weight(jax.random.fold_in(key_list[5], 71), 0),
        "out_weight": scatter_about(key_list[2], (D, D), D ** -0.5, 0.125, ((0, 8), (1, 4))),
        "neighbours": draw_neighbours(jax.random.fold_in(key_list[5], 71), 0),
        "counts": place_ends(jax.random.randint(key_list[4], (NBLK,), 7, 10), jax.random.fold_in(key_list[4], 1), 7, 9).astype(jnp.int32),
    }


def reference(tokens, qkv_weight, out_weight, neighbours, counts):
    usable = jnp.arange(NEIGH)[None, :] < counts[:, None]

    def one_head(head):
        panel = lax.dynamic_slice_in_dim(qkv_weight, (head * 3 * HEAD_WIDTH).astype(jnp.int32), 3 * HEAD_WIDTH, 1)
        projected = jnp.dot(tokens, panel, preferred_element_type=jnp.float32).astype(jnp.bfloat16)
        projected = projected.reshape(NBLK, BLK, 3, HEAD_WIDTH)
        query_matrix = projected[:, :, 0]
        neighbour_listing = projected[:, :, 1:][neighbours]
        attention_logits = jnp.einsum("azi,afci->azfc", query_matrix.astype(jnp.float32), neighbour_listing[..., 0, :].astype(jnp.float32)) * HEAD_WIDTH ** -0.5
        attention_logits = jnp.where(usable[:, None, :, None], attention_logits, -1e30)
        highest = jnp.max(attention_logits, axis=(2, 3), keepdims=True)
        expon = jnp.exp(attention_logits - highest)
        attention_probs = (expon / jnp.sum(expon, axis=(2, 3), keepdims=True)).astype(jnp.bfloat16)
        blended_values = jnp.einsum("mocs,mcsx->mox", attention_probs.astype(jnp.float32), neighbour_listing[..., 1, :].astype(jnp.float32)).astype(jnp.bfloat16)
        return blended_values.reshape(TOKENS, HEAD_WIDTH)

    heads = lax.map(one_head, jnp.arange(HEADS).astype(jnp.int32))
    blended_values = jnp.transpose(heads, (1, 0, 2)).reshape(TOKENS, D)
    return jnp.dot(blended_values, out_weight, preferred_element_type=jnp.float32).astype(jnp.bfloat16)
```

```python
import functools

import jax
import jax.numpy as jnp
from jax import lax
from jax.experimental import pallas as pl
from jax.experimental.pallas import tpu as pltpu
from jax.sharding import PartitionSpec as P

HEAD_WIDTH = 128
BLK = 64
NEIGH = 9
VMEM_LIMIT = 60 * 1024 * 1024
LOG2E = 1.4426950408889634


def line_gather(part, axis, size):
    to_right = [(i, i + 1) for i in range(size - 1)]
    to_left = [(i + 1, i) for i in range(size - 1)]
    left, right, from_left, from_right = part, part, [], []
    for _ in range(size - 1):
        left = lax.ppermute(left, axis, to_right)
        right = lax.ppermute(right, axis, to_left)
        from_left.append(left)
        from_right.append(right)
    return from_left, from_right


def exchange_gather(shard, axis, size):
    pieces = [shard] + [None] * (size - 1)
    for s in range(2, size, 2):
        pieces[s] = lax.ppermute(shard, axis, [(i, i ^ s) for i in range(size)])
    for s in range(0, size, 2):
        pieces[s + 1] = lax.ppermute(pieces[s], axis, [(i, i ^ 1) for i in range(size)])
    return pieces


def load_rows_parts(place, parts, dest, sem, hid_size, width):
    at_hid = place[0]
    chunks = len(parts)
    cut = width // chunks

    def each(act):
        for c, (own, from_left, from_right) in enumerate(parts):
            def copy(ref, source, k, c=c):
                begin = pl.multiple_of(source * width + c * cut, cut)
                return pltpu.make_async_copy(ref, dest.at[:, pl.ds(begin, cut)], sem.at[c, k])

            act(copy(own, at_hid, 0))
            for k in range(1, hid_size):
                @pl.when(at_hid >= k)
                def _():
                    act(copy(from_left[k - 1], at_hid - k, k))

                @pl.when(at_hid + k < hid_size)
                def _():
                    act(copy(from_right[k - 1], at_hid + k, hid_size - 1 + k))

    return (lambda: each(lambda d: d.start())), (lambda: each(lambda d: d.wait()))


def group_parts(refs, chunks, hid_size):
    per = 1 + 2 * (hid_size - 1)
    parts = []
    for c in range(chunks):
        r = refs[c * per : (c + 1) * per]
        parts.append((r[0], r[1 : hid_size], r[hid_size:]))
    return parts


def flat_parts(parts):
    return [x for own, a, b in parts for x in [own, *a, *b]]


def project_kernel(place, send_ids, *refs, chunks, hid_size, tok_size, width, columns, step, sends):
    n_parts = chunks * (1 + 2 * (hid_size - 1))
    parts = group_parts(refs[:n_parts], chunks, hid_size)
    pieces = refs[n_parts : n_parts + tok_size]
    outs = refs[n_parts + tok_size :]
    n_sends = tok_size - 1 if sends else 0
    result, send_refs = outs[0], outs[1 : 1 + n_sends]
    rows, weights, row_sem, weight_sem = outs[1 + n_sends :]
    at_tok = place[1]
    depth = pieces[0].shape[0]
    begin, total = columns
    start, wait = load_rows_parts(place, parts, rows, row_sem, hid_size, width)
    start()

    def weight_copy(s, n):
        at = pl.multiple_of((at_tok ^ s) * depth, depth)
        return pltpu.make_async_copy(
            pieces[s].at[:, pl.ds(begin + n * step, step)],
            weights.at[pl.ds(at, depth), pl.ds(n * step, step)],
            weight_sem.at[n, s],
        )

    steps = total // step
    for n in range(steps):
        for s in range(tok_size):
            weight_copy(s, n).start()
    wait()
    for n in range(steps):
        for s in range(tok_size):
            weight_copy(s, n).wait()
        result[:, n * step : (n + 1) * step] = jnp.dot(
            rows[...], weights[:, n * step : (n + 1) * step], preferred_element_type=jnp.float32
        ).astype(result.dtype)
    if sends:
        for s in range(1, tok_size):
            for slot in range(2):
                at = pl.multiple_of(send_ids[s, slot] * BLK, BLK)
                for j in range(total // (3 * HEAD_WIDTH)):
                    send_refs[s - 1][slot * BLK : (slot + 1) * BLK, j * 2 * HEAD_WIDTH : (j + 1) * 2 * HEAD_WIDTH] = (
                        result[pl.ds(at, BLK), (3 * j + 1) * HEAD_WIDTH : (3 * j + 3) * HEAD_WIDTH]
                    )


def project(place, send_ids, parts, pieces, columns, step, tok_size, hid_size, sends):
    chunks = len(parts)
    own = parts[0][0]
    tok_rows, width = own.shape[0], own.shape[1] * chunks
    full = width * hid_size
    total = columns[1]
    heads = total // (3 * HEAD_WIDTH)
    shapes = [jax.ShapeDtypeStruct((tok_rows, total), jnp.bfloat16)]
    if sends:
        shapes += [jax.ShapeDtypeStruct((2 * BLK, heads * 2 * HEAD_WIDTH), jnp.bfloat16)] * (tok_size - 1)
    flat = flat_parts(parts)
    return pl.pallas_call(
        functools.partial(
            project_kernel, chunks=chunks, hid_size=hid_size, tok_size=tok_size, width=width,
            columns=columns, step=step, sends=sends,
        ),
        out_shape=shapes,
        in_specs=[pl.BlockSpec(memory_space=pltpu.SMEM)] * 2
        + [pl.BlockSpec(memory_space=pl.ANY)] * (len(flat) + tok_size),
        out_specs=[pl.BlockSpec(memory_space=pltpu.VMEM)] * len(shapes),
        scratch_shapes=[
            pltpu.VMEM((tok_rows, full), jnp.bfloat16),
            pltpu.VMEM((full, total), jnp.bfloat16),
            pltpu.SemaphoreType.DMA((chunks, 2 * hid_size - 1)),
            pltpu.SemaphoreType.DMA((total // step, tok_size)),
        ],
        compiler_params=pltpu.CompilerParams(vmem_limit_bytes=VMEM_LIMIT),
        cost_estimate=pl.CostEstimate(
            flops=2 * tok_rows * full * total, bytes_accessed=2 * full * (tok_rows + total), transcendentals=0
        ),
    )(place, send_ids, *flat, *pieces)


def attend_kernel(lists, counts, projected, *refs, tok_size, heads):
    remote = refs[: tok_size - 1]
    result, pool, sem = refs[tok_size - 1 :]
    tok_rows = projected.shape[0]
    blocks = tok_rows // BLK
    pair = 2 * HEAD_WIDTH
    copies = []
    for j in range(heads):
        copies.append(pltpu.make_async_copy(
            projected.at[:, pl.ds((3 * j + 1) * HEAD_WIDTH, pair)],
            pool.at[pl.ds(0, tok_rows), pl.ds(j * pair, pair)],
            sem.at[tok_size - 1 + j],
        ))
    for s in range(tok_size - 1):
        copies.append(pltpu.make_async_copy(
            remote[s], pool.at[pl.ds(tok_rows + s * 2 * BLK, 2 * BLK), :], sem.at[s]
        ))
    for copy in copies:
        copy.start()
    for copy in copies:
        copy.wait()
    scale = HEAD_WIDTH ** (-0.5) * LOG2E

    def block(b, carry):
        at = pl.multiple_of(b * BLK, BLK)
        starts = [pl.multiple_of(lists[b, j] * BLK, BLK) for j in range(NEIGH)]
        limit = counts[b] * BLK
        usable = lax.broadcasted_iota(jnp.int32, (BLK, NEIGH * BLK), 1) < limit
        for h in range(heads):
            query = projected[pl.ds(at, BLK), 3 * h * HEAD_WIDTH : (3 * h + 1) * HEAD_WIDTH]
            keys = jnp.concatenate(
                [pool[pl.ds(i, BLK), h * pair : h * pair + HEAD_WIDTH] for i in starts], axis=0
            )
            logits = lax.dot_general(query, keys, (((1,), (1,)), ((), ())), preferred_element_type=jnp.float32)
            logits = jnp.where(usable, logits, -1e30)
            highest = jnp.max(logits, axis=1, keepdims=True)
            expon = jnp.exp2((logits - highest) * scale)
            total = jnp.sum(expon, axis=1, keepdims=True)
            values = jnp.concatenate(
                [pool[pl.ds(i, BLK), h * pair + HEAD_WIDTH : (h + 1) * pair] for i in starts], axis=0
            )
            blended = jnp.dot(expon.astype(jnp.bfloat16), values, preferred_element_type=jnp.float32)
            result[pl.ds(at, BLK), h * HEAD_WIDTH : (h + 1) * HEAD_WIDTH] = (blended / total).astype(result.dtype)
        return carry

    lax.fori_loop(0, blocks, block, 0)


def attend(lists, counts, projected, remote, tok_size):
    tok_rows = projected.shape[0]
    heads = projected.shape[1] // (3 * HEAD_WIDTH)
    return pl.pallas_call(
        functools.partial(attend_kernel, tok_size=tok_size, heads=heads),
        out_shape=jax.ShapeDtypeStruct((tok_rows, heads * HEAD_WIDTH), jnp.bfloat16),
        in_specs=[pl.BlockSpec(memory_space=pltpu.SMEM)] * 2
        + [pl.BlockSpec(memory_space=pltpu.VMEM)]
        + [pl.BlockSpec(memory_space=pl.ANY)] * (tok_size - 1),
        out_specs=pl.BlockSpec(memory_space=pltpu.VMEM),
        scratch_shapes=[
            pltpu.VMEM((tok_rows + (tok_size - 1) * 2 * BLK, heads * 2 * HEAD_WIDTH), jnp.bfloat16),
            pltpu.SemaphoreType.DMA((tok_size - 1 + heads,)),
        ],
        compiler_params=pltpu.CompilerParams(vmem_limit_bytes=VMEM_LIMIT),
        cost_estimate=pl.CostEstimate(
            flops=4 * tok_rows * NEIGH * BLK * HEAD_WIDTH * heads,
            bytes_accessed=4 * tok_rows * HEAD_WIDTH * heads * 8,
            transcendentals=tok_rows * NEIGH * BLK * heads,
        ),
    )(lists, counts, projected, *remote)


def routes(neighbours, counts, at_tok, tok_size, blocks):
    lists = neighbours.reshape(tok_size, blocks * NEIGH)
    valid = (jnp.arange(NEIGH)[None, :] < counts[:, None]).reshape(tok_size, blocks * NEIGH)
    owner = lists // blocks
    peers = jnp.arange(tok_size) ^ at_tok
    named = valid & (owner == at_tok)
    low = jnp.min(jnp.where(named, lists, tok_size * blocks), axis=1)
    high = jnp.max(jnp.where(named, lists, -1), axis=1)
    base = at_tok * blocks
    sends = jnp.clip(jnp.stack([low, high], axis=1) - base, 0, blocks - 1)
    send_ids = sends[peers]
    mine = lax.dynamic_slice_in_dim(lists, at_tok, 1, 0)[0]
    mine_valid = lax.dynamic_slice_in_dim(valid, at_tok, 1, 0)[0]
    mine_owner = mine // blocks
    same = (mine_owner[:, None] == mine_owner[None, :]) & mine_valid[None, :]
    first = jnp.min(jnp.where(same, mine[None, :], tok_size * blocks), axis=1)
    slot = (mine != first).astype(jnp.int32)
    there = blocks + ((mine_owner ^ at_tok) - 1) * 2 + slot
    pool_at = jnp.where(mine_owner == at_tok, mine - base, there)
    pool_at = jnp.where(mine_valid, pool_at, 0).reshape(blocks, NEIGH)
    my_counts = lax.dynamic_slice_in_dim(counts, at_tok * blocks, blocks, 0)
    return send_ids.astype(jnp.int32), pool_at.astype(jnp.int32), my_counts


def column_chunks(width):
    return 2 if width % (4 * HEAD_WIDTH) == 0 else 1


def shards(tokens, qkv_weight, out_weight, neighbours, counts, *, tok_size, hid_size):
    at_tok, at_hid = lax.axis_index("tok"), lax.axis_index("hid")
    blocks = tokens.shape[0] // BLK
    place = jnp.stack([at_hid, at_tok]).astype(jnp.int32)
    width = tokens.shape[1]
    chunks = column_chunks(width)
    cut = width // chunks
    parts = []
    for c in range(chunks):
        own = tokens[:, c * cut : (c + 1) * cut]
        parts.append((own, *line_gather(own, "hid", hid_size)))
    qkv_pieces = exchange_gather(qkv_weight, "tok", tok_size)
    out_pieces = exchange_gather(out_weight, "tok", tok_size)
    send_ids, pool_at, my_counts = routes(neighbours, counts, at_tok, tok_size, blocks)

    total = qkv_weight.shape[1]
    step = 256 if total % 256 == 0 else 128
    projected, *sends = project(
        place, send_ids, parts, qkv_pieces, (0, total), step, tok_size, hid_size, True
    )
    remote = [
        lax.ppermute(sends[s - 1], "tok", [(i, i ^ s) for i in range(tok_size)]) for s in range(1, tok_size)
    ]
    mixed = attend(pool_at, my_counts, projected, remote, tok_size)
    parts = []
    for c in range(chunks):
        own = mixed[:, c * cut : (c + 1) * cut]
        parts.append((own, *line_gather(own, "hid", hid_size)))
    out_columns = out_weight.shape[1]
    (result,) = project(
        place, send_ids, parts, out_pieces, (0, out_columns), min(256, out_columns), tok_size, hid_size, False
    )
    return result


def solution(mesh):
    placed = (P("tok", "hid"), P("tok", "hid"), P("tok", "hid"), P(), P())
    return jax.shard_map(
        functools.partial(shards, tok_size=mesh.shape["tok"], hid_size=mesh.shape["hid"]),
        mesh=mesh, in_specs=placed, out_specs=P("tok", "hid"), check_vma=False,
    )
```

```python
import functools

import jax
import jax.numpy as jnp
from jax import lax
from jax.experimental import pallas as pl
from jax.experimental.pallas import tpu as pltpu
from jax.sharding import PartitionSpec as P

HEAD_WIDTH = 128
BLK = 64
NEIGH = 9
MIB = 1024 * 1024
LOG2E = 1.4426950408889634
HBM = pl.BlockSpec(memory_space=pltpu.HBM)
SMEM = pl.BlockSpec(memory_space=pltpu.SMEM)
VMEM_LIMIT = 60 * MIB


def line_step(parts, axis, size):
    to_right = [(i, i + 1) for i in range(size - 1)]
    to_left = [(i + 1, i) for i in range(size - 1)]
    own, from_left, from_right = parts
    left = lax.ppermute((from_left or [own])[-1], axis, to_right)
    right = lax.ppermute((from_right or [own])[-1], axis, to_left)
    return own, from_left + [left], from_right + [right]


def swap(x, s, axis, size):
    return lax.ppermute(x, axis, [(i, i ^ s) for i in range(size)])


def tile_of(columns):
    return 256 if columns % 256 == 0 else 128


def accumulate_kernel(place, *refs, reach, hid_size, cut):
    chunks = len(reach)
    refs = list(refs)
    parts = []
    for c in range(chunks):
        own = refs.pop(0)
        from_left = [refs.pop(0) for _ in range(reach[c])]
        from_right = [refs.pop(0) for _ in range(reach[c])]
        parts.append((own, from_left, from_right))
    panel = refs.pop(0)
    total, last_rows, rows, weights, sums, row_sem, weight_sem, last_sem, sum_sem = refs
    at_hid = place[0]
    width = cut * chunks
    columns = total.shape[1]

    def each(act):
        for c, (own, from_left, from_right) in enumerate(parts):
            def copy(ref, source, k, c=c):
                at = pl.multiple_of(source * width + c * cut, cut)
                return pltpu.make_async_copy(ref, rows.at[:, pl.ds(at, cut)], row_sem.at[c, k])

            act(copy(own, at_hid, 0))
            for k in range(1, reach[c] + 1):
                @pl.when(at_hid >= k)
                def _():
                    act(copy(from_left[k - 1], at_hid - k, k))

                @pl.when(at_hid + k < hid_size)
                def _():
                    act(copy(from_right[k - 1], at_hid + k, hid_size - 1 + k))

    weight_copy = pltpu.make_async_copy(panel, weights, weight_sem)
    each(lambda d: d.start())
    weight_copy.start()
    for c in range(chunks):
        if reach[c] < hid_size - 1:
            for end, source in ((0, hid_size - 1), (hid_size - 1, 0)):
                @pl.when(at_hid == end)
                def _():
                    at = source * width + c * cut
                    rows[:, at : at + cut] = jnp.zeros((rows.shape[0], cut), rows.dtype)
    weight_copy.wait()
    source = jnp.where(at_hid == 0, hid_size - 1, 0)
    lasts = []
    for c in range(chunks):
        if reach[c] < hid_size - 1:
            at = pl.multiple_of(source * width + c * cut, cut)
            n = len(lasts)
            lasts.append(pltpu.make_async_copy(
                weights.at[pl.ds(at, cut), :], last_rows.at[pl.ds(n * cut, cut), :], last_sem.at[n]
            ))
    for copy in lasts:
        copy.start()
    each(lambda d: d.wait())
    step = tile_of(columns)
    for n in range(0, columns, step):
        sums[:, n : n + step] = jnp.dot(
            rows[...], weights[:, n : n + step], preferred_element_type=jnp.float32
        )
        lasts.append(pltpu.make_async_copy(
            sums.at[:, pl.ds(n, step)], total.at[:, pl.ds(n, step)], sum_sem.at[n // step]
        ))
        lasts[-1].start()
    for copy in lasts:
        copy.wait()


def accumulate(place, parts, panel, reach, hid_size):
    columns = panel.shape[1]
    chunks = len(parts)
    tok_rows, cut = parts[0][0].shape
    full = cut * chunks * hid_size
    flat = []
    for c, (own, from_left, from_right) in enumerate(parts):
        flat += [own, *from_left[: reach[c]], *from_right[: reach[c]]]
    deferred = sum(r < hid_size - 1 for r in reach)
    return pl.pallas_call(
        functools.partial(
            accumulate_kernel, reach=reach, hid_size=hid_size, cut=cut
        ),
        out_shape=[
            jax.ShapeDtypeStruct((tok_rows, columns), jnp.float32),
            jax.ShapeDtypeStruct((deferred * cut, columns), jnp.bfloat16),
        ],
        in_specs=[SMEM] + [HBM] * (len(flat) + 1),
        out_specs=[HBM, HBM],
        scratch_shapes=[
            pltpu.VMEM((tok_rows, full), jnp.bfloat16),
            pltpu.VMEM((full, columns), jnp.bfloat16),
            pltpu.VMEM((tok_rows, columns), jnp.float32),
            pltpu.SemaphoreType.DMA((chunks, 2 * hid_size - 1)),
            pltpu.SemaphoreType.DMA,
            pltpu.SemaphoreType.DMA((deferred,)),
            pltpu.SemaphoreType.DMA((columns // tile_of(columns),)),
        ],
        compiler_params=pltpu.CompilerParams(vmem_limit_bytes=VMEM_LIMIT),
        cost_estimate=pl.CostEstimate(
            flops=2 * tok_rows * full * columns, bytes_accessed=2 * full * (tok_rows + columns), transcendentals=0
        ),
    )(place, *flat, panel)


def finish_kernel(place, send_ids, *refs, deferred, hid_size, cut, begin, columns, n_sends):
    refs = list(refs)
    total = refs.pop(0)
    lasts = [(refs.pop(0), refs.pop(0)) for _ in range(deferred)]
    last_rows = refs.pop(0)
    n_outs = 2 + n_sends if n_sends else 1
    targets, outs, scratch = refs[:n_outs], refs[n_outs:-7], refs[-7:]
    sums, rows, weights, sum_sem, row_sem, weight_sem, out_sem = scratch
    at_hid = place[0]
    at_end = (at_hid == 0) | (at_hid == hid_size - 1)
    sum_copy = pltpu.make_async_copy(total.at[:, pl.ds(begin, columns)], sums, sum_sem)
    weight_copy = pltpu.make_async_copy(last_rows.at[:, pl.ds(begin, columns)], weights, weight_sem)
    sum_copy.start()

    def row_copies(side):
        return [
            pltpu.make_async_copy(lasts[c][side], rows.at[:, pl.ds(c * cut, cut)], row_sem.at[c])
            for c in range(deferred)
        ]

    for end, side in ((0, 1), (hid_size - 1, 0)):
        @pl.when(at_hid == end)
        def _():
            for copy in row_copies(side):
                copy.start()
            weight_copy.start()

    heads = columns // (3 * HEAD_WIDTH)

    def emit(n, value):
        if not n_sends:
            outs[0][:, n : n + value.shape[1]] = value
            return
        for g in range(n // HEAD_WIDTH, (n + value.shape[1]) // HEAD_WIDTH):
            piece = value[:, g * HEAD_WIDTH - n : (g + 1) * HEAD_WIDTH - n]
            head, kind = g // 3, g % 3
            target = outs[min(kind, 1)]
            at = ((kind == 2) * heads + head) * HEAD_WIDTH
            target[:, at : at + HEAD_WIDTH] = piece

    step = tile_of(columns)
    sum_copy.wait()

    @pl.when(at_end)
    def _():
        for copy in row_copies(0):
            copy.wait()
        weight_copy.wait()
        for n in range(0, columns, step):
            more = jnp.dot(rows[...], weights[:, n : n + step], preferred_element_type=jnp.float32)
            emit(n, (sums[:, n : n + step] + more).astype(jnp.bfloat16))

    @pl.when(jnp.logical_not(at_end))
    def _():
        for n in range(0, columns, step):
            emit(n, sums[:, n : n + step].astype(jnp.bfloat16))

    copies = []
    for s in range(n_sends):
        for slot in range(2):
            at = pl.multiple_of(send_ids[s + 1, slot] * BLK, BLK)
            copies.append(pltpu.make_async_copy(
                outs[1].at[pl.ds(at, BLK), :], targets[2 + s].at[pl.ds(slot * BLK, BLK), :],
                out_sem.at[2 + 2 * s + slot],
            ))
    for n, value in enumerate(outs):
        copies.append(pltpu.make_async_copy(value, targets[n], out_sem.at[n]))
    for copy in copies:
        copy.start()
    for copy in copies:
        copy.wait()


def finish(place, send_ids, total, lasts, last_rows, begin, columns, hid_size, n_sends):
    tok_rows = total.shape[0]
    deferred = len(lasts)
    cut = last_rows.shape[0] // deferred
    bf16 = lambda *shape: jax.ShapeDtypeStruct(shape, jnp.bfloat16)
    if n_sends:
        wide = columns // 3
        shapes = [bf16(tok_rows, wide), bf16(tok_rows, 2 * wide)] + [bf16(2 * BLK, 2 * wide)] * n_sends
    else:
        shapes = [bf16(tok_rows, columns)]
    flat = [x for pair in lasts for x in pair]
    return pl.pallas_call(
        functools.partial(
            finish_kernel, deferred=deferred, hid_size=hid_size, cut=cut, begin=begin, columns=columns,
            n_sends=n_sends,
        ),
        out_shape=shapes,
        in_specs=[SMEM] * 2 + [HBM] * (2 + len(flat)),
        out_specs=[HBM] * len(shapes),
        scratch_shapes=[pltpu.VMEM(x.shape, x.dtype) for x in shapes[:2]] + [
            pltpu.VMEM((tok_rows, columns), jnp.float32),
            pltpu.VMEM((tok_rows, deferred * cut), jnp.bfloat16),
            pltpu.VMEM((deferred * cut, columns), jnp.bfloat16),
            pltpu.SemaphoreType.DMA,
            pltpu.SemaphoreType.DMA((deferred,)),
            pltpu.SemaphoreType.DMA,
            pltpu.SemaphoreType.DMA((2 + 2 * n_sends,)),
        ],
        compiler_params=pltpu.CompilerParams(vmem_limit_bytes=VMEM_LIMIT),
        cost_estimate=pl.CostEstimate(
            flops=2 * tok_rows * deferred * cut * columns, bytes_accessed=8 * tok_rows * columns, transcendentals=0
        ),
    )(place, send_ids, total, *flat, last_rows)


def attend_kernel(lists, counts, query_all, key_values, *refs, tok_size, heads):
    remote = refs[: tok_size - 1]
    target, pool, queries, result, sem = refs[tok_size - 1 :]
    tok_rows = queries.shape[0]
    blocks = tok_rows // BLK
    wide = heads * HEAD_WIDTH
    copies = [
        pltpu.make_async_copy(key_values, pool.at[pl.ds(0, tok_rows), :], sem.at[tok_size - 1]),
        pltpu.make_async_copy(query_all, queries, sem.at[tok_size]),
    ]
    for s in range(tok_size - 1):
        copies.append(pltpu.make_async_copy(
            remote[s], pool.at[pl.ds(tok_rows + s * 2 * BLK, 2 * BLK), :], sem.at[s]
        ))
    for copy in copies:
        copy.start()
    for copy in copies:
        copy.wait()
    scale = HEAD_WIDTH ** (-0.5) * LOG2E
    diagonal = (
        lax.broadcasted_iota(jnp.int32, (heads * BLK, wide), 0) // BLK
        == lax.broadcasted_iota(jnp.int32, (heads * BLK, wide), 1) // HEAD_WIDTH
    )
    column = lax.broadcasted_iota(jnp.int32, (heads * BLK, NEIGH * BLK), 1)

    def block(b):
        at = pl.multiple_of(b * BLK, BLK)
        starts = [pl.multiple_of(lists[b, j] * BLK, BLK) for j in range(NEIGH)]
        query = jnp.concatenate([queries[pl.ds(at, BLK), :]] * heads, axis=0)
        query = jnp.where(diagonal, query, jnp.zeros_like(query))
        keys = jnp.concatenate([pool[pl.ds(i, BLK), :wide] for i in starts], axis=0)
        logits = lax.dot_general(query, keys, (((1,), (1,)), ((), ())), preferred_element_type=jnp.float32)
        logits = jnp.where(column < counts[b] * BLK, logits, -1e30)
        highest = jnp.max(logits, axis=1, keepdims=True)
        expon = jnp.exp2((logits - highest) * scale)
        total = jnp.sum(expon, axis=1, keepdims=True)
        values = jnp.concatenate([pool[pl.ds(i, BLK), wide:] for i in starts], axis=0)
        blended = jnp.dot(expon.astype(jnp.bfloat16), values, preferred_element_type=jnp.float32) / total
        for h in range(heads):
            own = slice(h * HEAD_WIDTH, (h + 1) * HEAD_WIDTH)
            result[pl.ds(at, BLK), own] = blended[h * BLK : (h + 1) * BLK, own].astype(result.dtype)

    unroll = next(u for u in (6, 4, 3, 2, 1) if blocks % u == 0)

    def body(i, carry):
        for u in range(unroll):
            block(i * unroll + u)
        return carry

    lax.fori_loop(0, blocks // unroll, body, 0)
    copy = pltpu.make_async_copy(result, target, sem.at[0])
    copy.start()
    copy.wait()


def attend(lists, counts, query, key_values, remote, tok_size):
    tok_rows, wide = query.shape
    heads = wide // HEAD_WIDTH
    return pl.pallas_call(
        functools.partial(attend_kernel, tok_size=tok_size, heads=heads),
        out_shape=jax.ShapeDtypeStruct((tok_rows, wide), jnp.bfloat16),
        in_specs=[SMEM] * 2 + [HBM] * (tok_size + 1),
        out_specs=HBM,
        scratch_shapes=[
            pltpu.VMEM((tok_rows + (tok_size - 1) * 2 * BLK, 2 * wide), jnp.bfloat16),
            pltpu.VMEM((tok_rows, wide), jnp.bfloat16),
            pltpu.VMEM((tok_rows, wide), jnp.bfloat16),
            pltpu.SemaphoreType.DMA((tok_size + 1,)),
        ],
        compiler_params=pltpu.CompilerParams(vmem_limit_bytes=VMEM_LIMIT),
        cost_estimate=pl.CostEstimate(
            flops=8 * tok_rows * NEIGH * BLK * wide,
            bytes_accessed=2 * tok_rows * wide * 10,
            transcendentals=tok_rows * NEIGH * BLK * heads,
        ),
    )(lists, counts, query, key_values, *remote)


def routes(neighbours, counts, at_tok, tok_size, blocks):
    lists = neighbours.reshape(tok_size, blocks * NEIGH)
    valid = (jnp.arange(NEIGH)[None, :] < counts[:, None]).reshape(tok_size, blocks * NEIGH)
    owner = lists // blocks
    peers = jnp.arange(tok_size) ^ at_tok
    named = valid & (owner == at_tok)
    low = jnp.min(jnp.where(named, lists, tok_size * blocks), axis=1)
    high = jnp.max(jnp.where(named, lists, -1), axis=1)
    base = at_tok * blocks
    sends = jnp.clip(jnp.stack([low, high], axis=1) - base, 0, blocks - 1)
    send_ids = sends[peers]
    mine = lax.dynamic_slice_in_dim(lists, at_tok, 1, 0)[0]
    mine_valid = lax.dynamic_slice_in_dim(valid, at_tok, 1, 0)[0]
    mine_owner = mine // blocks
    same = (mine_owner[:, None] == mine_owner[None, :]) & mine_valid[None, :]
    first = jnp.min(jnp.where(same, mine[None, :], tok_size * blocks), axis=1)
    slot = (mine != first).astype(jnp.int32)
    there = blocks + ((mine_owner ^ at_tok) - 1) * 2 + slot
    pool_at = jnp.where(mine_owner == at_tok, mine - base, there)
    pool_at = jnp.where(mine_valid, pool_at, 0).reshape(blocks, NEIGH)
    my_counts = lax.dynamic_slice_in_dim(counts, at_tok * blocks, blocks, 0)
    return send_ids.astype(jnp.int32), pool_at.astype(jnp.int32), my_counts


def shards(tokens, qkv_weight, out_weight, neighbours, counts, *, tok_size, hid_size):
    at_tok, at_hid = lax.axis_index("tok"), lax.axis_index("hid")
    blocks = tokens.shape[0] // BLK
    place = jnp.stack([at_hid, at_tok]).astype(jnp.int32)
    heads_here = qkv_weight.shape[1] // (3 * HEAD_WIDTH)
    group = 2 if heads_here % 2 == 0 else 1
    chunks = heads_here // group
    cut = group * HEAD_WIDTH
    far = hid_size - 1
    out_columns = out_weight.shape[1]

    qkv_panel = lax.all_gather(qkv_weight, "tok", axis=0, tiled=True)
    out_panel = lax.all_gather(out_weight, "tok", axis=0, tiled=True)
    parts = [(tokens[:, c * cut : (c + 1) * cut], [], []) for c in range(chunks)]
    parts = [line_step(p, "hid", hid_size) for p in parts]
    parts[-1], ids = lax.optimization_barrier(
        (parts[-1], routes(neighbours, counts, at_tok, tok_size, blocks))
    )
    send_ids, pool_at, my_counts = ids
    for _ in range(far - 1):
        parts = [line_step(p, "hid", hid_size) for p in parts]

    total, last_rows = accumulate(place, parts, qkv_panel, [far - 1] * chunks, hid_size)
    lasts = [(from_left[-1], from_right[-1]) for _, from_left, from_right in parts]
    parts, remote = [], []
    for c in range(chunks):
        columns = 3 * cut
        query, key_values, *sends = finish(
            place, send_ids, total, lasts, last_rows, c * columns, columns, hid_size, tok_size - 1
        )
        sends, remote = lax.optimization_barrier((sends, remote))
        remote = [swap(sends[s - 1], s, "tok", tok_size) for s in range(1, tok_size)]
        if parts:
            remote, _ = lax.optimization_barrier((remote, parts[-1][0]))
        mixed = attend(pool_at, my_counts, query, key_values, remote, tok_size)
        part = (mixed, [], [])
        for _ in range(far):
            part = line_step(part, "hid", hid_size)
        parts.append(part)
    total, last_rows = accumulate(place, parts, out_panel, [far - 1] * chunks, hid_size)
    lasts = [(from_left[-1], from_right[-1]) for _, from_left, from_right in parts]
    (result,) = finish(place, send_ids, total, lasts, last_rows, 0, out_columns, hid_size, 0)
    return result


def solution(mesh):
    placed = (P("tok", "hid"), P("tok", "hid"), P("tok", "hid"), P(), P())
    return jax.shard_map(
        functools.partial(shards, tok_size=mesh.shape["tok"], hid_size=mesh.shape["hid"]),
        mesh=mesh, in_specs=placed, out_specs=P("tok", "hid"), check_vma=False,
    )
```

```python
import functools

import jax
import jax.numpy as jnp
from jax import lax
from jax.experimental import pallas as pl
from jax.experimental.pallas import tpu as pltpu
from jax.sharding import PartitionSpec as P

HEAD_WIDTH = 128
BLK = 64
NEIGH = 9
MIB = 1024 * 1024
LOG2E = 1.4426950408889634
HBM = pl.BlockSpec(memory_space=pltpu.HBM)
SMEM = pl.BlockSpec(memory_space=pltpu.SMEM)
VMEM_LIMIT = 60 * MIB


def line_step(parts, axis, size):
    to_right = [(i, i + 1) for i in range(size - 1)]
    to_left = [(i + 1, i) for i in range(size - 1)]
    own, from_left, from_right = parts
    left = lax.ppermute((from_left or [own])[-1], axis, to_right)
    right = lax.ppermute((from_right or [own])[-1], axis, to_left)
    return own, from_left + [left], from_right + [right]


def swap(x, s, axis, size):
    return lax.ppermute(x, axis, [(i, i ^ s) for i in range(size)])


def halves(x):
    return [x[: x.shape[0] // 2], x[x.shape[0] // 2 :]]


def forward(pieces, s, axis, size):
    a = s & -s
    b = s ^ a
    via_a, via_b = sum(map(halves, pieces[b]), [])[:2], sum(map(halves, pieces[a]), [])[-2:]
    if len(pieces[b]) > 1 or len(pieces[a]) > 1:
        return [swap(x, a, axis, size) for x in pieces[b]]
    return [swap(via_a[0], a, axis, size), swap(via_b[-1], b, axis, size)]


def tile_of(columns):
    return 256 if columns % 256 == 0 else 128


def accumulate_kernel(place, *refs, reach, hid_size, layout, arrays, cut):
    chunks = len(reach)
    refs = list(refs)
    parts = []
    for c in range(chunks):
        own = refs.pop(0)
        from_left = [refs.pop(0) for _ in range(reach[c])]
        from_right = [refs.pop(0) for _ in range(reach[c])]
        parts.append((own, from_left, from_right))
    stacks = [refs.pop(0) for _ in range(arrays)]
    tok_size = len(layout)
    total, last_rows, rows, weights, sums, row_sem, weight_sem, last_sem, sum_sem = refs
    at_hid, at_tok = place[0], place[1]
    width = cut * chunks
    depth = sum(n for _, _, n in layout[0])
    columns = total.shape[1]

    def each(act):
        for c, (own, from_left, from_right) in enumerate(parts):
            def copy(ref, source, k, c=c):
                at = pl.multiple_of(source * width + c * cut, cut)
                return pltpu.make_async_copy(ref, rows.at[:, pl.ds(at, cut)], row_sem.at[c, k])

            act(copy(own, at_hid, 0))
            for k in range(1, reach[c] + 1):
                @pl.when(at_hid >= k)
                def _():
                    act(copy(from_left[k - 1], at_hid - k, k))

                @pl.when(at_hid + k < hid_size)
                def _():
                    act(copy(from_right[k - 1], at_hid + k, hid_size - 1 + k))

    weight_copies = []
    for s in range(tok_size):
        at = (at_tok ^ s) * depth
        for array, first, n in layout[s]:
            here = pl.ds(pl.multiple_of(at, n), n)
            weight_copies.append(pltpu.make_async_copy(
                stacks[array].at[pl.ds(first, n), :], weights.at[here, :], weight_sem.at[len(weight_copies)]
            ))
            at = at + n

    each(lambda d: d.start())
    for copy in weight_copies:
        copy.start()
    for c in range(chunks):
        if reach[c] < hid_size - 1:
            for end, source in ((0, hid_size - 1), (hid_size - 1, 0)):
                @pl.when(at_hid == end)
                def _():
                    at = source * width + c * cut
                    rows[:, at : at + cut] = jnp.zeros((rows.shape[0], cut), rows.dtype)
    for copy in weight_copies:
        copy.wait()
    source = jnp.where(at_hid == 0, hid_size - 1, 0)
    lasts = []
    for c in range(chunks):
        if reach[c] < hid_size - 1:
            at = pl.multiple_of(source * width + c * cut, cut)
            n = len(lasts)
            lasts.append(pltpu.make_async_copy(
                weights.at[pl.ds(at, cut), :], last_rows.at[pl.ds(n * cut, cut), :], last_sem.at[n]
            ))
    for copy in lasts:
        copy.start()
    each(lambda d: d.wait())
    step = tile_of(columns)
    for n in range(0, columns, step):
        sums[:, n : n + step] = jnp.dot(
            rows[...], weights[:, n : n + step], preferred_element_type=jnp.float32
        )
        lasts.append(pltpu.make_async_copy(
            sums.at[:, pl.ds(n, step)], total.at[:, pl.ds(n, step)], sum_sem.at[n // step]
        ))
        lasts[-1].start()
    for copy in lasts:
        copy.wait()


def accumulate(place, parts, stacks, layout, reach, hid_size):
    columns = stacks[0].shape[1]
    copies = sum(map(len, layout))
    chunks = len(parts)
    tok_rows, cut = parts[0][0].shape
    full = cut * chunks * hid_size
    flat = []
    for c, (own, from_left, from_right) in enumerate(parts):
        flat += [own, *from_left[: reach[c]], *from_right[: reach[c]]]
    deferred = sum(r < hid_size - 1 for r in reach)
    return pl.pallas_call(
        functools.partial(
            accumulate_kernel, reach=reach, hid_size=hid_size, layout=layout,
            arrays=len(stacks), cut=cut,
        ),
        out_shape=[
            jax.ShapeDtypeStruct((tok_rows, columns), jnp.float32),
            jax.ShapeDtypeStruct((deferred * cut, columns), jnp.bfloat16),
        ],
        in_specs=[SMEM] + [HBM] * (len(flat) + len(stacks)),
        out_specs=[HBM, HBM],
        scratch_shapes=[
            pltpu.VMEM((tok_rows, full), jnp.bfloat16),
            pltpu.VMEM((full, columns), jnp.bfloat16),
            pltpu.VMEM((tok_rows, columns), jnp.float32),
            pltpu.SemaphoreType.DMA((chunks, 2 * hid_size - 1)),
            pltpu.SemaphoreType.DMA((copies,)),
            pltpu.SemaphoreType.DMA((deferred,)),
            pltpu.SemaphoreType.DMA((columns // tile_of(columns),)),
        ],
        compiler_params=pltpu.CompilerParams(vmem_limit_bytes=VMEM_LIMIT),
        cost_estimate=pl.CostEstimate(
            flops=2 * tok_rows * full * columns, bytes_accessed=2 * full * (tok_rows + columns), transcendentals=0
        ),
    )(place, *flat, *stacks)


def finish_kernel(place, send_ids, *refs, deferred, hid_size, cut, begin, columns, n_sends):
    refs = list(refs)
    total = refs.pop(0)
    lasts = [(refs.pop(0), refs.pop(0)) for _ in range(deferred)]
    last_rows = refs.pop(0)
    n_outs = 2 + n_sends if n_sends else 1
    targets, outs, scratch = refs[:n_outs], refs[n_outs:-7], refs[-7:]
    sums, rows, weights, sum_sem, row_sem, weight_sem, out_sem = scratch
    at_hid = place[0]
    at_end = (at_hid == 0) | (at_hid == hid_size - 1)
    sum_copy = pltpu.make_async_copy(total.at[:, pl.ds(begin, columns)], sums, sum_sem)
    weight_copy = pltpu.make_async_copy(last_rows.at[:, pl.ds(begin, columns)], weights, weight_sem)
    sum_copy.start()

    def row_copies(side):
        return [
            pltpu.make_async_copy(lasts[c][side], rows.at[:, pl.ds(c * cut, cut)], row_sem.at[c])
            for c in range(deferred)
        ]

    for end, side in ((0, 1), (hid_size - 1, 0)):
        @pl.when(at_hid == end)
        def _():
            for copy in row_copies(side):
                copy.start()
            weight_copy.start()

    heads = columns // (3 * HEAD_WIDTH)

    def emit(n, value):
        if not n_sends:
            outs[0][:, n : n + value.shape[1]] = value
            return
        for g in range(n // HEAD_WIDTH, (n + value.shape[1]) // HEAD_WIDTH):
            piece = value[:, g * HEAD_WIDTH - n : (g + 1) * HEAD_WIDTH - n]
            head, kind = g // 3, g % 3
            target = outs[min(kind, 1)]
            at = ((kind == 2) * heads + head) * HEAD_WIDTH
            target[:, at : at + HEAD_WIDTH] = piece

    step = tile_of(columns)
    sum_copy.wait()

    @pl.when(at_end)
    def _():
        for copy in row_copies(0):
            copy.wait()
        weight_copy.wait()
        for n in range(0, columns, step):
            more = jnp.dot(rows[...], weights[:, n : n + step], preferred_element_type=jnp.float32)
            emit(n, (sums[:, n : n + step] + more).astype(jnp.bfloat16))

    @pl.when(jnp.logical_not(at_end))
    def _():
        for n in range(0, columns, step):
            emit(n, sums[:, n : n + step].astype(jnp.bfloat16))

    copies = []
    for i in range(n_sends):
        for slot in range(targets[2 + i].shape[0] // BLK):
            peer = place[1] ^ (1 if i == 0 else 2 * i + slot // 2)
            at = pl.multiple_of(send_ids[peer, slot % 2] * BLK, BLK)
            copies.append(pltpu.make_async_copy(
                outs[1].at[pl.ds(at, BLK), :], targets[2 + i].at[pl.ds(slot * BLK, BLK), :],
                out_sem.at[2 + len(copies)],
            ))
    for n, value in enumerate(outs):
        copies.append(pltpu.make_async_copy(value, targets[n], out_sem.at[n]))
    for copy in copies:
        copy.start()
    for copy in copies:
        copy.wait()


def finish(place, send_ids, total, lasts, last_rows, begin, columns, hid_size, n_sends):
    tok_rows = total.shape[0]
    deferred = len(lasts)
    cut = last_rows.shape[0] // deferred
    bf16 = lambda *shape: jax.ShapeDtypeStruct(shape, jnp.bfloat16)
    if n_sends:
        wide = columns // 3
        shapes = [bf16(tok_rows, wide), bf16(tok_rows, 2 * wide)] + [bf16((2 if i == 0 else 4) * BLK, 2 * wide) for i in range(n_sends)]
    else:
        shapes = [bf16(tok_rows, columns)]
    flat = [x for pair in lasts for x in pair]
    return pl.pallas_call(
        functools.partial(
            finish_kernel, deferred=deferred, hid_size=hid_size, cut=cut, begin=begin, columns=columns,
            n_sends=n_sends,
        ),
        out_shape=shapes,
        in_specs=[SMEM] * 2 + [HBM] * (2 + len(flat)),
        out_specs=[HBM] * len(shapes),
        scratch_shapes=[pltpu.VMEM(x.shape, x.dtype) for x in shapes[:2]] + [
            pltpu.VMEM((tok_rows, columns), jnp.float32),
            pltpu.VMEM((tok_rows, deferred * cut), jnp.bfloat16),
            pltpu.VMEM((deferred * cut, columns), jnp.bfloat16),
            pltpu.SemaphoreType.DMA,
            pltpu.SemaphoreType.DMA((deferred,)),
            pltpu.SemaphoreType.DMA,
            pltpu.SemaphoreType.DMA((2 + 4 * n_sends,)),
        ],
        compiler_params=pltpu.CompilerParams(vmem_limit_bytes=VMEM_LIMIT),
        cost_estimate=pl.CostEstimate(
            flops=2 * tok_rows * deferred * cut * columns, bytes_accessed=8 * tok_rows * columns, transcendentals=0
        ),
    )(place, send_ids, total, *flat, last_rows)


def attend_kernel(place, lists, counts, query_all, key_values, *refs, tok_size, heads):
    passed, remote = refs[0], refs[1 : tok_size // 2]
    target, pool, queries, result, sem = refs[tok_size // 2 :]
    tok_rows = queries.shape[0]
    blocks = tok_rows // BLK
    wide = heads * HEAD_WIDTH
    copies = [
        pltpu.make_async_copy(key_values, pool.at[pl.ds(0, tok_rows), :], sem.at[tok_size - 1]),
        pltpu.make_async_copy(query_all, queries, sem.at[tok_size]),
    ]
    for s in range(1, tok_size):
        ref = passed.at[pl.ds((s // 2) * 2 * BLK, 2 * BLK), :] if s % 2 else remote[s // 2 - 1].at[pl.ds(0, 2 * BLK), :]
        copies.append(pltpu.make_async_copy(
            ref, pool.at[pl.ds(tok_rows + (s - 1) * 2 * BLK, 2 * BLK), :], sem.at[s - 1]
        ))
    for copy in copies:
        copy.start()
    for copy in copies:
        copy.wait()
    scale = HEAD_WIDTH ** (-0.5) * LOG2E
    diagonal = (
        lax.broadcasted_iota(jnp.int32, (heads * BLK, wide), 0) // BLK
        == lax.broadcasted_iota(jnp.int32, (heads * BLK, wide), 1) // HEAD_WIDTH
    )
    column = lax.broadcasted_iota(jnp.int32, (heads * BLK, NEIGH * BLK), 1)

    def block(b):
        at = pl.multiple_of(b * BLK, BLK)
        starts = [pl.multiple_of(lists[0, b * NEIGH + j] * BLK, BLK) for j in range(NEIGH)]
        query = jnp.concatenate([queries[pl.ds(at, BLK), :]] * heads, axis=0)
        query = jnp.where(diagonal, query, jnp.zeros_like(query))
        keys = jnp.concatenate([pool[pl.ds(i, BLK), :wide] for i in starts], axis=0)
        logits = lax.dot_general(query, keys, (((1,), (1,)), ((), ())), preferred_element_type=jnp.float32)
        logits = jnp.where(column < counts[place[1] * blocks + b] * BLK, logits, -1e30)
        highest = jnp.max(logits, axis=1, keepdims=True)
        expon = jnp.exp2((logits - highest) * scale)
        total = jnp.sum(expon, axis=1, keepdims=True)
        values = jnp.concatenate([pool[pl.ds(i, BLK), wide:] for i in starts], axis=0)
        blended = jnp.dot(expon.astype(jnp.bfloat16), values, preferred_element_type=jnp.float32) / total
        for h in range(heads):
            own = slice(h * HEAD_WIDTH, (h + 1) * HEAD_WIDTH)
            result[pl.ds(at, BLK), own] = blended[h * BLK : (h + 1) * BLK, own].astype(result.dtype)

    unroll = next(u for u in (6, 4, 3, 2, 1) if blocks % u == 0)

    def body(i, carry):
        for u in range(unroll):
            block(i * unroll + u)
        return carry

    lax.fori_loop(0, blocks // unroll, body, 0)
    copy = pltpu.make_async_copy(result, target, sem.at[0])
    copy.start()
    copy.wait()


def attend(place, lists, counts, query, key_values, remote, tok_size):
    tok_rows, wide = query.shape
    heads = wide // HEAD_WIDTH
    return pl.pallas_call(
        functools.partial(attend_kernel, tok_size=tok_size, heads=heads),
        out_shape=jax.ShapeDtypeStruct((tok_rows, wide), jnp.bfloat16),
        in_specs=[SMEM] * 3 + [HBM] * (2 + tok_size // 2),
        out_specs=HBM,
        scratch_shapes=[
            pltpu.VMEM((tok_rows + (tok_size - 1) * 2 * BLK, 2 * wide), jnp.bfloat16),
            pltpu.VMEM((tok_rows, wide), jnp.bfloat16),
            pltpu.VMEM((tok_rows, wide), jnp.bfloat16),
            pltpu.SemaphoreType.DMA((tok_size + 1,)),
        ],
        compiler_params=pltpu.CompilerParams(vmem_limit_bytes=VMEM_LIMIT),
        cost_estimate=pl.CostEstimate(
            flops=8 * tok_rows * NEIGH * BLK * wide,
            bytes_accessed=2 * tok_rows * wide * 10,
            transcendentals=tok_rows * NEIGH * BLK * heads,
        ),
    )(place, lists, counts, query, key_values, *remote)


def routes_kernel(place, lists_ref, send_ids, pool_at, *, blocks):
    at_tok = place[1]
    tok_size = lists_ref.shape[0]
    lists = lists_ref[...]
    base = at_tok * blocks
    named = (lists >= base) & (lists < base + blocks)
    low = jnp.min(jnp.where(named, lists - base, blocks - 1), axis=1, keepdims=True)
    high = jnp.max(jnp.where(named, lists - base, 0), axis=1, keepdims=True)
    side = lax.broadcasted_iota(jnp.int32, send_ids.shape, 1)
    send_ids[...] = jnp.where(side == 0, low, high)
    mine = lists_ref[pl.ds(at_tok, 1), :]
    at = jnp.where((mine >= base) & (mine < base + blocks), mine - base, 0)
    for p in range(tok_size):
        here = (mine >= p * blocks) & (mine < (p + 1) * blocks)
        first = jnp.min(jnp.where(here, mine, tok_size * blocks), axis=1, keepdims=True)
        there = blocks + ((at_tok ^ p) - 1) * 2 + (mine != first).astype(jnp.int32)
        at = jnp.where(here & (p != at_tok), there, at)
    pool_at[...] = at


def routes(place, neighbours, counts, tok_size, blocks):
    usable = jnp.arange(NEIGH)[None, :] < counts[:, None]
    lists = jnp.where(usable, neighbours, -1).reshape(tok_size, blocks * NEIGH)
    vmem = pl.BlockSpec(memory_space=pltpu.VMEM)
    return pl.pallas_call(
        functools.partial(routes_kernel, blocks=blocks),
        out_shape=[
            jax.ShapeDtypeStruct((tok_size, 128), jnp.int32),
            jax.ShapeDtypeStruct((1, blocks * NEIGH), jnp.int32),
        ],
        in_specs=[SMEM, vmem],
        out_specs=[vmem, vmem],
    )(place, lists)


def shards(tokens, qkv_weight, out_weight, neighbours, counts, *, tok_size, hid_size):
    at_tok, at_hid = lax.axis_index("tok"), lax.axis_index("hid")
    blocks = tokens.shape[0] // BLK
    place = jnp.stack([at_hid, at_tok]).astype(jnp.int32)
    heads_here = qkv_weight.shape[1] // (3 * HEAD_WIDTH)
    group = 2 if heads_here % 2 == 0 else 1
    chunks = heads_here // group
    cut = group * HEAD_WIDTH
    far = hid_size - 1
    out_columns = out_weight.shape[1]

    weight = qkv_weight
    near = [s for s in range(2, tok_size) if s & (s - 1) == 0]
    even = range(0, tok_size, 2)
    pieces = [[weight]] + [None] * (tok_size - 1)
    part = line_step((tokens, [], []), "hid", hid_size)
    for s in near:
        pieces[s] = [swap(weight, s, "tok", tok_size)]
    part, (send_ids, pool_at) = lax.optimization_barrier(
        (part, routes(place, neighbours, counts, tok_size, blocks))
    )
    bits = [1 << i for i in reversed(range(tok_size.bit_length() - 1))]
    out_rows, out_ids = out_weight, [0]
    for bit in bits[:-2]:
        came = swap(out_rows, bit, "tok", tok_size)
        came, held = lax.optimization_barrier((came, [pieces[s] for s in near]))
        for s, piece in zip(near, held):
            pieces[s] = piece
        out_rows, out_ids = jnp.concatenate([out_rows, came], axis=0), out_ids + [s ^ bit for s in out_ids]
    came = swap(out_rows, 2, "tok", tok_size)
    for _ in range(far - 1):
        part = line_step(part, "hid", hid_size)
    for s in even:
        if pieces[s] is None:
            pieces[s] = forward(pieces, s, "tok", tok_size)
    held = lax.optimization_barrier([pieces[s] for s in even])
    for s, piece in zip(even, held):
        pieces[s + 1] = [swap(x, 1, "tok", tok_size) for x in piece]
    parts = [part]

    stacks, layout = [], []
    for piece in pieces:
        layout.append([(len(stacks) + i, 0, x.shape[0]) for i, x in enumerate(piece)])
        stacks += piece
    total, last_rows = accumulate(place, parts, stacks, layout, [far - 1], hid_size)
    total, came = lax.optimization_barrier((total, came))
    out_rows, out_ids = jnp.concatenate([out_rows, came], axis=0), out_ids + [s ^ 2 for s in out_ids]
    came = swap(out_rows, 1, "tok", tok_size)
    lasts = [(from_left[-1], from_right[-1]) for _, from_left, from_right in parts]
    groups = [
        finish(place, send_ids, total, lasts, last_rows, c * 3 * cut, 3 * cut, hid_size, tok_size // 2)
        for c in range(chunks)
    ]
    parts = []
    for c in range(chunks):
        query, key_values, *sends = groups[c]
        remote = [swap(sends[i], 2 * i, "tok", tok_size) for i in range(1, tok_size // 2)]
        remote, groups[c + 1 :], _ = lax.optimization_barrier(
            (remote, groups[c + 1 :], [p[0] for p in parts])
        )
        passed = jnp.concatenate([sends[0]] + [x[2 * BLK :] for x in remote], axis=0)
        remote = [swap(passed, 1, "tok", tok_size)] + remote
        mixed = attend(place, pool_at, counts, query, key_values, remote, tok_size)
        part = (mixed, [], [])
        for _ in range(far):
            part = line_step(part, "hid", hid_size)
        parts.append(part)
    depth = out_weight.shape[0]
    layout = [[(s not in out_ids, out_ids.index(s if s in out_ids else s ^ 1) * depth, depth)] for s in range(tok_size)]
    layout = [[(int(a), first, n)] for ((a, first, n),) in layout]
    total, last_rows = accumulate(place, parts, [out_rows, came], layout, [far - 1] * chunks, hid_size)
    lasts = [(from_left[-1], from_right[-1]) for _, from_left, from_right in parts]
    (result,) = finish(place, send_ids, total, lasts, last_rows, 0, out_columns, hid_size, 0)
    return result


def solution(mesh):
    placed = (P("tok", "hid"), P("tok", "hid"), P("tok", "hid"), P(), P())
    return jax.shard_map(
        functools.partial(shards, tok_size=mesh.shape["tok"], hid_size=mesh.shape["hid"]),
        mesh=mesh, in_specs=placed, out_specs=P("tok", "hid"), check_vma=False,
    )
```

```python
import functools

import jax
import jax.numpy as jnp
from jax import lax
from jax.experimental import pallas as pl
from jax.experimental.pallas import tpu as pltpu
from jax.sharding import PartitionSpec as P

HEAD_WIDTH = 128
BLK = 64
NEIGH = 9
MIB = 1024 * 1024
LOG2E = 1.4426950408889634
HBM = pl.BlockSpec(memory_space=pltpu.HBM)
SMEM = pl.BlockSpec(memory_space=pltpu.SMEM)
VMEM_LIMIT = 60 * MIB


def line_step(parts, axis, size):
    to_right = [(i, i + 1) for i in range(size - 1)]
    to_left = [(i + 1, i) for i in range(size - 1)]
    own, from_left, from_right = parts
    left = lax.ppermute((from_left or [own])[-1], axis, to_right)
    right = lax.ppermute((from_right or [own])[-1], axis, to_left)
    return own, from_left + [left], from_right + [right]


def swap(x, s, axis, size):
    return lax.ppermute(x, axis, [(i, i ^ s) for i in range(size)])


def halves(x):
    return [x[: x.shape[0] // 2], x[x.shape[0] // 2 :]]


def forward(pieces, s, axis, size):
    a = s & -s
    b = s ^ a
    via_a, via_b = sum(map(halves, pieces[b]), [])[:2], sum(map(halves, pieces[a]), [])[-2:]
    if len(pieces[b]) > 1 or len(pieces[a]) > 1:
        return [swap(x, a, axis, size) for x in pieces[b]]
    return [swap(via_a[0], a, axis, size), swap(via_b[-1], b, axis, size)]


def tile_of(columns):
    return 256 if columns % 256 == 0 else 128


def accumulate_kernel(place, *refs, reach, hid_size, layout, arrays, cut):
    chunks = len(reach)
    refs = list(refs)
    parts = []
    for c in range(chunks):
        own = refs.pop(0)
        from_left = [refs.pop(0) for _ in range(reach[c])]
        from_right = [refs.pop(0) for _ in range(reach[c])]
        parts.append((own, from_left, from_right))
    stacks = [refs.pop(0) for _ in range(arrays)]
    tok_size = len(layout)
    total, last_rows, rows, weights, sums, row_sem, weight_sem, last_sem, sum_sem = refs
    at_hid, at_tok = place[0], place[1]
    width = cut * chunks
    depth = sum(n for _, _, n in layout[0])
    columns = total.shape[1]

    def each(act):
        for c, (own, from_left, from_right) in enumerate(parts):
            def copy(ref, source, k, c=c):
                at = pl.multiple_of(source * width + c * cut, cut)
                return pltpu.make_async_copy(ref, rows.at[:, pl.ds(at, cut)], row_sem.at[c, k])

            act(copy(own, at_hid, 0))
            for k in range(1, reach[c] + 1):
                @pl.when(at_hid >= k)
                def _():
                    act(copy(from_left[k - 1], at_hid - k, k))

                @pl.when(at_hid + k < hid_size)
                def _():
                    act(copy(from_right[k - 1], at_hid + k, hid_size - 1 + k))

    weight_copies = []
    for s in range(tok_size):
        at = (at_tok ^ s) * depth
        for array, first, n in layout[s]:
            here = pl.ds(pl.multiple_of(at, n), n)
            weight_copies.append(pltpu.make_async_copy(
                stacks[array].at[pl.ds(first, n), :], weights.at[here, :], weight_sem.at[len(weight_copies)]
            ))
            at = at + n

    each(lambda d: d.start())
    for copy in weight_copies:
        copy.start()
    for c in range(chunks):
        if reach[c] < hid_size - 1:
            for end, source in ((0, hid_size - 1), (hid_size - 1, 0)):
                @pl.when(at_hid == end)
                def _():
                    at = source * width + c * cut
                    rows[:, at : at + cut] = jnp.zeros((rows.shape[0], cut), rows.dtype)
    for copy in weight_copies:
        copy.wait()
    source = jnp.where(at_hid == 0, hid_size - 1, 0)
    lasts = []
    for c in range(chunks):
        if reach[c] < hid_size - 1:
            at = pl.multiple_of(source * width + c * cut, cut)
            n = len(lasts)
            lasts.append(pltpu.make_async_copy(
                weights.at[pl.ds(at, cut), :], last_rows.at[pl.ds(n * cut, cut), :], last_sem.at[n]
            ))
    for copy in lasts:
        copy.start()
    each(lambda d: d.wait())
    step = tile_of(columns)
    for n in range(0, columns, step):
        sums[:, n : n + step] = jnp.dot(
            rows[...], weights[:, n : n + step], preferred_element_type=jnp.float32
        )
        lasts.append(pltpu.make_async_copy(
            sums.at[:, pl.ds(n, step)], total.at[:, pl.ds(n, step)], sum_sem.at[n // step]
        ))
        lasts[-1].start()
    for copy in lasts:
        copy.wait()


def accumulate(place, parts, stacks, layout, reach, hid_size):
    columns = stacks[0].shape[1]
    copies = sum(map(len, layout))
    chunks = len(parts)
    tok_rows, cut = parts[0][0].shape
    full = cut * chunks * hid_size
    flat = []
    for c, (own, from_left, from_right) in enumerate(parts):
        flat += [own, *from_left[: reach[c]], *from_right[: reach[c]]]
    deferred = sum(r < hid_size - 1 for r in reach)
    return pl.pallas_call(
        functools.partial(
            accumulate_kernel, reach=reach, hid_size=hid_size, layout=layout,
            arrays=len(stacks), cut=cut,
        ),
        out_shape=[
            jax.ShapeDtypeStruct((tok_rows, columns), jnp.float32),
            jax.ShapeDtypeStruct((deferred * cut, columns), jnp.bfloat16),
        ],
        in_specs=[SMEM] + [HBM] * (len(flat) + len(stacks)),
        out_specs=[HBM, HBM],
        scratch_shapes=[
            pltpu.VMEM((tok_rows, full), jnp.bfloat16),
            pltpu.VMEM((full, columns), jnp.bfloat16),
            pltpu.VMEM((tok_rows, columns), jnp.float32),
            pltpu.SemaphoreType.DMA((chunks, 2 * hid_size - 1)),
            pltpu.SemaphoreType.DMA((copies,)),
            pltpu.SemaphoreType.DMA((deferred,)),
            pltpu.SemaphoreType.DMA((columns // tile_of(columns),)),
        ],
        compiler_params=pltpu.CompilerParams(vmem_limit_bytes=VMEM_LIMIT),
        cost_estimate=pl.CostEstimate(
            flops=2 * tok_rows * full * columns, bytes_accessed=2 * full * (tok_rows + columns), transcendentals=0
        ),
    )(place, *flat, *stacks)


def finish_kernel(place, send_ids, *refs, deferred, hid_size, cut, begin, columns, n_sends):
    refs = list(refs)
    total = refs.pop(0)
    lasts = [(refs.pop(0), refs.pop(0)) for _ in range(deferred)]
    last_rows = refs.pop(0)
    n_outs = 2 + n_sends if n_sends else 1
    targets, outs, scratch = refs[:n_outs], refs[n_outs:-7], refs[-7:]
    sums, rows, weights, sum_sem, row_sem, weight_sem, out_sem = scratch
    at_hid = place[0]
    at_end = (at_hid == 0) | (at_hid == hid_size - 1)
    sum_copy = pltpu.make_async_copy(total.at[:, pl.ds(begin, columns)], sums, sum_sem)
    weight_copy = pltpu.make_async_copy(last_rows.at[:, pl.ds(begin, columns)], weights, weight_sem)
    sum_copy.start()

    def row_copies(side):
        return [
            pltpu.make_async_copy(lasts[c][side], rows.at[:, pl.ds(c * cut, cut)], row_sem.at[c])
            for c in range(deferred)
        ]

    for end, side in ((0, 1), (hid_size - 1, 0)):
        @pl.when(at_hid == end)
        def _():
            for copy in row_copies(side):
                copy.start()
            weight_copy.start()

    heads = columns // (3 * HEAD_WIDTH)

    def emit(n, value):
        if not n_sends:
            outs[0][:, n : n + value.shape[1]] = value
            return
        for g in range(n // HEAD_WIDTH, (n + value.shape[1]) // HEAD_WIDTH):
            piece = value[:, g * HEAD_WIDTH - n : (g + 1) * HEAD_WIDTH - n]
            head, kind = g // 3, g % 3
            target = outs[min(kind, 1)]
            at = ((kind == 2) * heads + head) * HEAD_WIDTH
            target[:, at : at + HEAD_WIDTH] = piece

    step = tile_of(columns)
    sum_copy.wait()

    @pl.when(at_end)
    def _():
        for copy in row_copies(0):
            copy.wait()
        weight_copy.wait()
        for n in range(0, columns, step):
            more = jnp.dot(rows[...], weights[:, n : n + step], preferred_element_type=jnp.float32)
            emit(n, (sums[:, n : n + step] + more).astype(jnp.bfloat16))

    @pl.when(jnp.logical_not(at_end))
    def _():
        for n in range(0, columns, step):
            emit(n, sums[:, n : n + step].astype(jnp.bfloat16))

    copies = []
    for i in range(n_sends):
        for slot in range(targets[2 + i].shape[0] // BLK):
            peer = place[1] ^ (1 if i == 0 else 2 * i + slot // 2)
            at = pl.multiple_of(send_ids[peer, slot % 2] * BLK, BLK)
            copies.append(pltpu.make_async_copy(
                outs[1].at[pl.ds(at, BLK), :], targets[2 + i].at[pl.ds(slot * BLK, BLK), :],
                out_sem.at[2 + len(copies)],
            ))
    for n, value in enumerate(outs):
        copies.append(pltpu.make_async_copy(value, targets[n], out_sem.at[n]))
    for copy in copies:
        copy.start()
    for copy in copies:
        copy.wait()


def finish(place, send_ids, total, lasts, last_rows, begin, columns, hid_size, n_sends):
    tok_rows = total.shape[0]
    deferred = len(lasts)
    cut = last_rows.shape[0] // deferred
    bf16 = lambda *shape: jax.ShapeDtypeStruct(shape, jnp.bfloat16)
    if n_sends:
        wide = columns // 3
        shapes = [bf16(tok_rows, wide), bf16(tok_rows, 2 * wide)] + [bf16((2 if i == 0 else 4) * BLK, 2 * wide) for i in range(n_sends)]
    else:
        shapes = [bf16(tok_rows, columns)]
    flat = [x for pair in lasts for x in pair]
    return pl.pallas_call(
        functools.partial(
            finish_kernel, deferred=deferred, hid_size=hid_size, cut=cut, begin=begin, columns=columns,
            n_sends=n_sends,
        ),
        out_shape=shapes,
        in_specs=[SMEM] * 2 + [HBM] * (2 + len(flat)),
        out_specs=[HBM] * len(shapes),
        scratch_shapes=[pltpu.VMEM(x.shape, x.dtype) for x in shapes[:2]] + [
            pltpu.VMEM((tok_rows, columns), jnp.float32),
            pltpu.VMEM((tok_rows, deferred * cut), jnp.bfloat16),
            pltpu.VMEM((deferred * cut, columns), jnp.bfloat16),
            pltpu.SemaphoreType.DMA,
            pltpu.SemaphoreType.DMA((deferred,)),
            pltpu.SemaphoreType.DMA,
            pltpu.SemaphoreType.DMA((2 + 4 * n_sends,)),
        ],
        compiler_params=pltpu.CompilerParams(vmem_limit_bytes=VMEM_LIMIT),
        cost_estimate=pl.CostEstimate(
            flops=2 * tok_rows * deferred * cut * columns, bytes_accessed=8 * tok_rows * columns, transcendentals=0
        ),
    )(place, send_ids, total, *flat, last_rows)


def attend_kernel(place, lists, counts, query_all, key_values, *refs, tok_size, heads):
    passed, remote = refs[0], refs[1 : tok_size // 2]
    target, pool, queries, result, sem = refs[tok_size // 2 :]
    tok_rows = queries.shape[0]
    blocks = tok_rows // BLK
    wide = heads * HEAD_WIDTH
    copies = [
        pltpu.make_async_copy(key_values, pool.at[pl.ds(0, tok_rows), :], sem.at[tok_size - 1]),
        pltpu.make_async_copy(query_all, queries, sem.at[tok_size]),
    ]
    for s in range(1, tok_size):
        ref = passed.at[pl.ds((s // 2) * 2 * BLK, 2 * BLK), :] if s % 2 else remote[s // 2 - 1].at[pl.ds(0, 2 * BLK), :]
        copies.append(pltpu.make_async_copy(
            ref, pool.at[pl.ds(tok_rows + (s - 1) * 2 * BLK, 2 * BLK), :], sem.at[s - 1]
        ))
    for copy in copies:
        copy.start()
    for copy in copies:
        copy.wait()
    scale = HEAD_WIDTH ** (-0.5) * LOG2E
    diagonal = (
        lax.broadcasted_iota(jnp.int32, (heads * BLK, wide), 0) // BLK
        == lax.broadcasted_iota(jnp.int32, (heads * BLK, wide), 1) // HEAD_WIDTH
    )
    column = lax.broadcasted_iota(jnp.int32, (heads * BLK, NEIGH * BLK), 1)

    def block(b):
        at = pl.multiple_of(b * BLK, BLK)
        starts = [pl.multiple_of(lists[0, b * NEIGH + j] * BLK, BLK) for j in range(NEIGH)]
        query = jnp.concatenate([queries[pl.ds(at, BLK), :]] * heads, axis=0)
        query = jnp.where(diagonal, query, jnp.zeros_like(query))
        keys = jnp.concatenate([pool[pl.ds(i, BLK), :wide] for i in starts], axis=0)
        logits = lax.dot_general(query, keys, (((1,), (1,)), ((), ())), preferred_element_type=jnp.float32)
        logits = jnp.where(column < counts[place[1] * blocks + b] * BLK, logits, -1e30)
        highest = jnp.max(logits, axis=1, keepdims=True)
        expon = jnp.exp2((logits - highest) * scale)
        total = jnp.sum(expon, axis=1, keepdims=True)
        values = jnp.concatenate([pool[pl.ds(i, BLK), wide:] for i in starts], axis=0)
        blended = jnp.dot(expon.astype(jnp.bfloat16), values, preferred_element_type=jnp.float32) / total
        for h in range(heads):
            own = slice(h * HEAD_WIDTH, (h + 1) * HEAD_WIDTH)
            result[pl.ds(at, BLK), own] = blended[h * BLK : (h + 1) * BLK, own].astype(result.dtype)

    unroll = next(u for u in (6, 4, 3, 2, 1) if blocks % u == 0)

    def body(i, carry):
        for u in range(unroll):
            block(i * unroll + u)
        return carry

    lax.fori_loop(0, blocks // unroll, body, 0)
    copy = pltpu.make_async_copy(result, target, sem.at[0])
    copy.start()
    copy.wait()


def attend(place, lists, counts, query, key_values, remote, tok_size):
    tok_rows, wide = query.shape
    heads = wide // HEAD_WIDTH
    return pl.pallas_call(
        functools.partial(attend_kernel, tok_size=tok_size, heads=heads),
        out_shape=jax.ShapeDtypeStruct((tok_rows, wide), jnp.bfloat16),
        in_specs=[SMEM] * 3 + [HBM] * (2 + tok_size // 2),
        out_specs=HBM,
        scratch_shapes=[
            pltpu.VMEM((tok_rows + (tok_size - 1) * 2 * BLK, 2 * wide), jnp.bfloat16),
            pltpu.VMEM((tok_rows, wide), jnp.bfloat16),
            pltpu.VMEM((tok_rows, wide), jnp.bfloat16),
            pltpu.SemaphoreType.DMA((tok_size + 1,)),
        ],
        compiler_params=pltpu.CompilerParams(vmem_limit_bytes=VMEM_LIMIT),
        cost_estimate=pl.CostEstimate(
            flops=8 * tok_rows * NEIGH * BLK * wide,
            bytes_accessed=2 * tok_rows * wide * 10,
            transcendentals=tok_rows * NEIGH * BLK * heads,
        ),
    )(place, lists, counts, query, key_values, *remote)


def routes_kernel(place, lists_ref, send_ids, pool_at, *, blocks):
    at_tok = place[1]
    tok_size = lists_ref.shape[0]
    lists = lists_ref[...]
    base = at_tok * blocks
    named = (lists >= base) & (lists < base + blocks)
    low = jnp.min(jnp.where(named, lists - base, blocks - 1), axis=1, keepdims=True)
    high = jnp.max(jnp.where(named, lists - base, 0), axis=1, keepdims=True)
    side = lax.broadcasted_iota(jnp.int32, send_ids.shape, 1)
    send_ids[...] = jnp.where(side == 0, low, high)
    mine = lists_ref[pl.ds(at_tok, 1), :]
    at = jnp.where((mine >= base) & (mine < base + blocks), mine - base, 0)
    for p in range(tok_size):
        here = (mine >= p * blocks) & (mine < (p + 1) * blocks)
        first = jnp.min(jnp.where(here, mine, tok_size * blocks), axis=1, keepdims=True)
        there = blocks + ((at_tok ^ p) - 1) * 2 + (mine != first).astype(jnp.int32)
        at = jnp.where(here & (p != at_tok), there, at)
    pool_at[...] = at


def routes(place, neighbours, counts, tok_size, blocks):
    usable = jnp.arange(NEIGH)[None, :] < counts[:, None]
    lists = jnp.where(usable, neighbours, -1).reshape(tok_size, blocks * NEIGH)
    vmem = pl.BlockSpec(memory_space=pltpu.VMEM)
    return pl.pallas_call(
        functools.partial(routes_kernel, blocks=blocks),
        out_shape=[
            jax.ShapeDtypeStruct((tok_size, 128), jnp.int32),
            jax.ShapeDtypeStruct((1, blocks * NEIGH), jnp.int32),
        ],
        in_specs=[SMEM, vmem],
        out_specs=[vmem, vmem],
    )(place, lists)


def shards(tokens, qkv_weight, out_weight, neighbours, counts, *, tok_size, hid_size):
    at_tok, at_hid = lax.axis_index("tok"), lax.axis_index("hid")
    blocks = tokens.shape[0] // BLK
    place = jnp.stack([at_hid, at_tok]).astype(jnp.int32)
    heads_here = qkv_weight.shape[1] // (3 * HEAD_WIDTH)
    group = 2 if heads_here % 2 == 0 else 1
    chunks = heads_here // group
    cut = group * HEAD_WIDTH
    far = hid_size - 1
    out_columns = out_weight.shape[1]

    weight = qkv_weight
    near = [s for s in range(2, tok_size) if s & (s - 1) == 0]
    even = range(0, tok_size, 2)
    pieces = [[weight]] + [None] * (tok_size - 1)
    part = line_step((tokens, [], []), "hid", hid_size)
    for s in near:
        pieces[s] = [swap(weight, s, "tok", tok_size)]
    send_ids, pool_at = routes(place, neighbours, counts, tok_size, blocks)
    bits = [1 << i for i in reversed(range(tok_size.bit_length() - 1))]
    out_rows, out_ids = out_weight, [0]
    for bit in bits[:-2]:
        came = swap(out_rows, bit, "tok", tok_size)
        out_rows, out_ids = jnp.concatenate([out_rows, came], axis=0), out_ids + [s ^ bit for s in out_ids]
    came = swap(out_rows, 2, "tok", tok_size)
    for _ in range(far - 1):
        part = line_step(part, "hid", hid_size)
    for s in even:
        if pieces[s] is None:
            pieces[s] = forward(pieces, s, "tok", tok_size)
    for s in even:
        pieces[s + 1] = [swap(x, 1, "tok", tok_size) for x in pieces[s]]
    parts = [part]

    stacks, layout = [], []
    for piece in pieces:
        layout.append([(len(stacks) + i, 0, x.shape[0]) for i, x in enumerate(piece)])
        stacks += piece
    total, last_rows = accumulate(place, parts, stacks, layout, [far - 1], hid_size)
    total, came, send_ids, pool_at = lax.optimization_barrier((total, came, send_ids, pool_at))
    out_rows, out_ids = jnp.concatenate([out_rows, came], axis=0), out_ids + [s ^ 2 for s in out_ids]
    came = swap(out_rows, 1, "tok", tok_size)
    lasts = [(from_left[-1], from_right[-1]) for _, from_left, from_right in parts]
    groups = [
        finish(place, send_ids, total, lasts, last_rows, c * 3 * cut, 3 * cut, hid_size, tok_size // 2)
        for c in range(chunks)
    ]
    parts = []
    for c in range(chunks):
        query, key_values, *sends = groups[c]
        remote = [swap(sends[i], 2 * i, "tok", tok_size) for i in range(1, tok_size // 2)]
        remote, groups[c + 1 :], _ = lax.optimization_barrier(
            (remote, groups[c + 1 :], [p[0] for p in parts])
        )
        passed = jnp.concatenate([sends[0]] + [x[2 * BLK :] for x in remote], axis=0)
        remote = [swap(passed, 1, "tok", tok_size)] + remote
        mixed = attend(place, pool_at, counts, query, key_values, remote, tok_size)
        part = (mixed, [], [])
        for _ in range(far):
            part = line_step(part, "hid", hid_size)
        parts.append(part)
    depth = out_weight.shape[0]
    layout = [[(s not in out_ids, out_ids.index(s if s in out_ids else s ^ 1) * depth, depth)] for s in range(tok_size)]
    layout = [[(int(a), first, n)] for ((a, first, n),) in layout]
    total, last_rows = accumulate(place, parts, [out_rows, came], layout, [far - 1] * chunks, hid_size)
    lasts = [(from_left[-1], from_right[-1]) for _, from_left, from_right in parts]
    (result,) = finish(place, send_ids, total, lasts, last_rows, 0, out_columns, hid_size, 0)
    return result


def solution(mesh):
    placed = (P("tok", "hid"), P("tok", "hid"), P("tok", "hid"), P(), P())
    return jax.shard_map(
        functools.partial(shards, tok_size=mesh.shape["tok"], hid_size=mesh.shape["hid"]),
        mesh=mesh, in_specs=placed, out_specs=P("tok", "hid"), check_vma=False,
    )
```

```python
import functools

import jax
import jax.numpy as jnp
from jax import lax
from jax.experimental import pallas as pl
from jax.experimental.pallas import tpu as pltpu
from jax.sharding import PartitionSpec as P

HEAD_WIDTH = 128
BLK = 64
NEIGH = 9
MIB = 1024 * 1024
LOG2E = 1.4426950408889634
HBM = pl.BlockSpec(memory_space=pltpu.HBM)
ANY = pl.BlockSpec(memory_space=pl.ANY)
SMEM = pl.BlockSpec(memory_space=pltpu.SMEM)
VMEM_LIMIT = 60 * MIB


def line_step(parts, axis, size):
    to_right = [(i, i + 1) for i in range(size - 1)]
    to_left = [(i + 1, i) for i in range(size - 1)]
    own, from_left, from_right = parts
    left = lax.ppermute((from_left or [own])[-1], axis, to_right)
    right = lax.ppermute((from_right or [own])[-1], axis, to_left)
    return own, from_left + [left], from_right + [right]


def swap(x, s, axis, size):
    return lax.ppermute(x, axis, [(i, i ^ s) for i in range(size)])


def halves(x):
    return [x[: x.shape[0] // 2], x[x.shape[0] // 2 :]]


def forward(pieces, s, axis, size):
    a = s & -s
    b = s ^ a
    via_a, via_b = sum(map(halves, pieces[b]), [])[:2], sum(map(halves, pieces[a]), [])[-2:]
    if len(pieces[b]) > 1 or len(pieces[a]) > 1:
        return [swap(x, a, axis, size) for x in pieces[b]]
    return [swap(via_a[0], a, axis, size), swap(via_b[-1], b, axis, size)]


def tile_of(columns):
    return 256 if columns % 256 == 0 else 128


def accumulate_kernel(place, *refs, reach, hid_size, layout, arrays, cut):
    chunks = len(reach)
    refs = list(refs)
    parts = []
    for c in range(chunks):
        own = refs.pop(0)
        from_left = [refs.pop(0) for _ in range(reach[c])]
        from_right = [refs.pop(0) for _ in range(reach[c])]
        parts.append((own, from_left, from_right))
    stacks = [refs.pop(0) for _ in range(arrays)]
    tok_size = len(layout)
    total, last_rows, rows, weights, sums, row_sem, weight_sem, last_sem, sum_sem = refs
    at_hid, at_tok = place[0], place[1]
    width = cut * chunks
    depth = sum(n for _, _, n in layout[0])
    columns = total.shape[1]

    def each(act):
        for c, (own, from_left, from_right) in enumerate(parts):
            def copy(ref, source, k, c=c):
                at = pl.multiple_of(source * width + c * cut, cut)
                return pltpu.make_async_copy(ref, rows.at[:, pl.ds(at, cut)], row_sem.at[c, k])

            act(copy(own, at_hid, 0))
            for k in range(1, reach[c] + 1):
                @pl.when(at_hid >= k)
                def _():
                    act(copy(from_left[k - 1], at_hid - k, k))

                @pl.when(at_hid + k < hid_size)
                def _():
                    act(copy(from_right[k - 1], at_hid + k, hid_size - 1 + k))

    weight_copies = []
    for s in range(tok_size):
        at = (at_tok ^ s) * depth
        for array, first, n in layout[s]:
            here = pl.ds(pl.multiple_of(at, n), n)
            weight_copies.append(pltpu.make_async_copy(
                stacks[array].at[pl.ds(first, n), :], weights.at[here, :], weight_sem.at[len(weight_copies)]
            ))
            at = at + n

    each(lambda d: d.start())
    for copy in weight_copies:
        copy.start()
    for c in range(chunks):
        if reach[c] < hid_size - 1:
            for end, source in ((0, hid_size - 1), (hid_size - 1, 0)):
                @pl.when(at_hid == end)
                def _():
                    at = source * width + c * cut
                    rows[:, at : at + cut] = jnp.zeros((rows.shape[0], cut), rows.dtype)
    for copy in weight_copies:
        copy.wait()
    source = jnp.where(at_hid == 0, hid_size - 1, 0)
    lasts = []
    for c in range(chunks):
        if reach[c] < hid_size - 1:
            at = pl.multiple_of(source * width + c * cut, cut)
            n = len(lasts)
            lasts.append(pltpu.make_async_copy(
                weights.at[pl.ds(at, cut), :], last_rows.at[pl.ds(n * cut, cut), :], last_sem.at[n]
            ))
    for copy in lasts:
        copy.start()
    each(lambda d: d.wait())
    step = tile_of(columns)
    for n in range(0, columns, step):
        sums[:, n : n + step] = jnp.dot(
            rows[...], weights[:, n : n + step], preferred_element_type=jnp.float32
        )
        lasts.append(pltpu.make_async_copy(
            sums.at[:, pl.ds(n, step)], total.at[:, pl.ds(n, step)], sum_sem.at[n // step]
        ))
        lasts[-1].start()
    for copy in lasts:
        copy.wait()


def accumulate(place, parts, stacks, layout, reach, hid_size):
    columns = stacks[0].shape[1]
    copies = sum(map(len, layout))
    chunks = len(parts)
    tok_rows, cut = parts[0][0].shape
    full = cut * chunks * hid_size
    flat = []
    for c, (own, from_left, from_right) in enumerate(parts):
        flat += [own, *from_left[: reach[c]], *from_right[: reach[c]]]
    deferred = sum(r < hid_size - 1 for r in reach)
    return pl.pallas_call(
        functools.partial(
            accumulate_kernel, reach=reach, hid_size=hid_size, layout=layout,
            arrays=len(stacks), cut=cut,
        ),
        out_shape=[
            jax.ShapeDtypeStruct((tok_rows, columns), jnp.float32),
            jax.ShapeDtypeStruct((deferred * cut, columns), jnp.bfloat16),
        ],
        in_specs=[SMEM] + [ANY] * (len(flat) + len(stacks)),
        out_specs=[HBM, HBM],
        scratch_shapes=[
            pltpu.VMEM((tok_rows, full), jnp.bfloat16),
            pltpu.VMEM((full, columns), jnp.bfloat16),
            pltpu.VMEM((tok_rows, columns), jnp.float32),
            pltpu.SemaphoreType.DMA((chunks, 2 * hid_size - 1)),
            pltpu.SemaphoreType.DMA((copies,)),
            pltpu.SemaphoreType.DMA((deferred,)),
            pltpu.SemaphoreType.DMA((columns // tile_of(columns),)),
        ],
        compiler_params=pltpu.CompilerParams(vmem_limit_bytes=VMEM_LIMIT),
        cost_estimate=pl.CostEstimate(
            flops=2 * tok_rows * full * columns, bytes_accessed=2 * full * (tok_rows + columns), transcendentals=0
        ),
    )(place, *flat, *stacks)


def finish_kernel(place, send_ids, *refs, deferred, hid_size, cut, begin, columns, n_sends):
    refs = list(refs)
    total = refs.pop(0)
    lasts = [(refs.pop(0), refs.pop(0)) for _ in range(deferred)]
    last_rows = refs.pop(0)
    n_outs = 2 + n_sends if n_sends else 1
    targets, outs, scratch = refs[:n_outs], refs[n_outs:-7], refs[-7:]
    sums, rows, weights, sum_sem, row_sem, weight_sem, out_sem = scratch
    at_hid = place[0]
    at_end = (at_hid == 0) | (at_hid == hid_size - 1)
    sum_copy = pltpu.make_async_copy(total.at[:, pl.ds(begin, columns)], sums, sum_sem)
    weight_copy = pltpu.make_async_copy(last_rows.at[:, pl.ds(begin, columns)], weights, weight_sem)
    sum_copy.start()

    def row_copies(side):
        return [
            pltpu.make_async_copy(lasts[c][side], rows.at[:, pl.ds(c * cut, cut)], row_sem.at[c])
            for c in range(deferred)
        ]

    for end, side in ((0, 1), (hid_size - 1, 0)):
        @pl.when(at_hid == end)
        def _():
            for copy in row_copies(side):
                copy.start()
            weight_copy.start()

    heads = columns // (3 * HEAD_WIDTH)

    def emit(n, value):
        if not n_sends:
            outs[0][:, n : n + value.shape[1]] = value
            return
        for g in range(n // HEAD_WIDTH, (n + value.shape[1]) // HEAD_WIDTH):
            piece = value[:, g * HEAD_WIDTH - n : (g + 1) * HEAD_WIDTH - n]
            head, kind = g // 3, g % 3
            target = outs[min(kind, 1)]
            at = ((kind == 2) * heads + head) * HEAD_WIDTH
            target[:, at : at + HEAD_WIDTH] = piece

    step = tile_of(columns)
    sum_copy.wait()

    @pl.when(at_end)
    def _():
        for copy in row_copies(0):
            copy.wait()
        weight_copy.wait()
        for n in range(0, columns, step):
            more = jnp.dot(rows[...], weights[:, n : n + step], preferred_element_type=jnp.float32)
            emit(n, (sums[:, n : n + step] + more).astype(jnp.bfloat16))

    @pl.when(jnp.logical_not(at_end))
    def _():
        for n in range(0, columns, step):
            emit(n, sums[:, n : n + step].astype(jnp.bfloat16))

    copies = []
    for i in range(n_sends):
        for slot in range(targets[2 + i].shape[0] // BLK):
            peer = place[1] ^ (1 if i == 0 else 2 * i + slot // 2)
            at = pl.multiple_of(send_ids[peer, slot % 2] * BLK, BLK)
            copies.append(pltpu.make_async_copy(
                outs[1].at[pl.ds(at, BLK), :], targets[2 + i].at[pl.ds(slot * BLK, BLK), :],
                out_sem.at[2 + len(copies)],
            ))
    for n, value in enumerate(outs):
        copies.append(pltpu.make_async_copy(value, targets[n], out_sem.at[n]))
    for copy in copies:
        copy.start()
    for copy in copies:
        copy.wait()


def finish(place, send_ids, total, lasts, last_rows, begin, columns, hid_size, n_sends):
    tok_rows = total.shape[0]
    deferred = len(lasts)
    cut = last_rows.shape[0] // deferred
    bf16 = lambda *shape: jax.ShapeDtypeStruct(shape, jnp.bfloat16)
    if n_sends:
        wide = columns // 3
        shapes = [bf16(tok_rows, wide), bf16(tok_rows, 2 * wide)] + [bf16((2 if i == 0 else 4) * BLK, 2 * wide) for i in range(n_sends)]
    else:
        shapes = [bf16(tok_rows, columns)]
    flat = [x for pair in lasts for x in pair]
    return pl.pallas_call(
        functools.partial(
            finish_kernel, deferred=deferred, hid_size=hid_size, cut=cut, begin=begin, columns=columns,
            n_sends=n_sends,
        ),
        out_shape=shapes,
        in_specs=[SMEM] * 2 + [HBM] * (2 + len(flat)),
        out_specs=[HBM] * len(shapes),
        scratch_shapes=[pltpu.VMEM(x.shape, x.dtype) for x in shapes[:2]] + [
            pltpu.VMEM((tok_rows, columns), jnp.float32),
            pltpu.VMEM((tok_rows, deferred * cut), jnp.bfloat16),
            pltpu.VMEM((deferred * cut, columns), jnp.bfloat16),
            pltpu.SemaphoreType.DMA,
            pltpu.SemaphoreType.DMA((deferred,)),
            pltpu.SemaphoreType.DMA,
            pltpu.SemaphoreType.DMA((2 + 4 * n_sends,)),
        ],
        compiler_params=pltpu.CompilerParams(vmem_limit_bytes=VMEM_LIMIT),
        cost_estimate=pl.CostEstimate(
            flops=2 * tok_rows * deferred * cut * columns, bytes_accessed=8 * tok_rows * columns, transcendentals=0
        ),
    )(place, send_ids, total, *flat, last_rows)


def attend_kernel(place, lists, counts, query_all, key_values, *refs, tok_size, heads):
    passed, remote = refs[0], refs[1 : tok_size // 2]
    target, pool, queries, result, sem = refs[tok_size // 2 :]
    tok_rows = queries.shape[0]
    blocks = tok_rows // BLK
    wide = heads * HEAD_WIDTH
    copies = [
        pltpu.make_async_copy(key_values, pool.at[pl.ds(0, tok_rows), :], sem.at[tok_size - 1]),
        pltpu.make_async_copy(query_all, queries, sem.at[tok_size]),
    ]
    for s in range(1, tok_size):
        ref = passed.at[pl.ds((s // 2) * 2 * BLK, 2 * BLK), :] if s % 2 else remote[s // 2 - 1].at[pl.ds(0, 2 * BLK), :]
        copies.append(pltpu.make_async_copy(
            ref, pool.at[pl.ds(tok_rows + (s - 1) * 2 * BLK, 2 * BLK), :], sem.at[s - 1]
        ))
    for copy in copies:
        copy.start()
    for copy in copies:
        copy.wait()
    scale = HEAD_WIDTH ** (-0.5) * LOG2E
    diagonal = (
        lax.broadcasted_iota(jnp.int32, (heads * BLK, wide), 0) // BLK
        == lax.broadcasted_iota(jnp.int32, (heads * BLK, wide), 1) // HEAD_WIDTH
    )
    column = lax.broadcasted_iota(jnp.int32, (heads * BLK, NEIGH * BLK), 1)

    def block(b):
        at = pl.multiple_of(b * BLK, BLK)
        starts = [pl.multiple_of(lists[0, b * NEIGH + j] * BLK, BLK) for j in range(NEIGH)]
        query = jnp.concatenate([queries[pl.ds(at, BLK), :]] * heads, axis=0)
        query = jnp.where(diagonal, query, jnp.zeros_like(query))
        keys = jnp.concatenate([pool[pl.ds(i, BLK), :wide] for i in starts], axis=0)
        logits = lax.dot_general(query, keys, (((1,), (1,)), ((), ())), preferred_element_type=jnp.float32)
        logits = jnp.where(column < counts[place[1] * blocks + b] * BLK, logits, -1e30)
        highest = jnp.max(logits, axis=1, keepdims=True)
        expon = jnp.exp2((logits - highest) * scale)
        total = jnp.sum(expon, axis=1, keepdims=True)
        values = jnp.concatenate([pool[pl.ds(i, BLK), wide:] for i in starts], axis=0)
        blended = jnp.dot(expon.astype(jnp.bfloat16), values, preferred_element_type=jnp.float32) / total
        for h in range(heads):
            own = slice(h * HEAD_WIDTH, (h + 1) * HEAD_WIDTH)
            result[pl.ds(at, BLK), own] = blended[h * BLK : (h + 1) * BLK, own].astype(result.dtype)

    unroll = next(u for u in (6, 4, 3, 2, 1) if blocks % u == 0)

    def body(i, carry):
        for u in range(unroll):
            block(i * unroll + u)
        return carry

    lax.fori_loop(0, blocks // unroll, body, 0)
    copy = pltpu.make_async_copy(result, target, sem.at[0])
    copy.start()
    copy.wait()


def attend(place, lists, counts, query, key_values, remote, tok_size):
    tok_rows, wide = query.shape
    heads = wide // HEAD_WIDTH
    return pl.pallas_call(
        functools.partial(attend_kernel, tok_size=tok_size, heads=heads),
        out_shape=jax.ShapeDtypeStruct((tok_rows, wide), jnp.bfloat16),
        in_specs=[SMEM] * 3 + [ANY] * (2 + tok_size // 2),
        out_specs=HBM,
        scratch_shapes=[
            pltpu.VMEM((tok_rows + (tok_size - 1) * 2 * BLK, 2 * wide), jnp.bfloat16),
            pltpu.VMEM((tok_rows, wide), jnp.bfloat16),
            pltpu.VMEM((tok_rows, wide), jnp.bfloat16),
            pltpu.SemaphoreType.DMA((tok_size + 1,)),
        ],
        compiler_params=pltpu.CompilerParams(vmem_limit_bytes=16 * MIB),
        cost_estimate=pl.CostEstimate(
            flops=8 * tok_rows * NEIGH * BLK * wide,
            bytes_accessed=2 * tok_rows * wide * 10,
            transcendentals=tok_rows * NEIGH * BLK * heads,
        ),
    )(place, lists, counts, query, key_values, *remote)


def routes_kernel(place, lists_ref, send_ids, pool_at, *, blocks):
    at_tok = place[1]
    tok_size = lists_ref.shape[0]
    lists = lists_ref[...]
    base = at_tok * blocks
    named = (lists >= base) & (lists < base + blocks)
    low = jnp.min(jnp.where(named, lists - base, blocks - 1), axis=1, keepdims=True)
    high = jnp.max(jnp.where(named, lists - base, 0), axis=1, keepdims=True)
    side = lax.broadcasted_iota(jnp.int32, send_ids.shape, 1)
    send_ids[...] = jnp.where(side == 0, low, high)
    mine = lists_ref[pl.ds(at_tok, 1), :]
    at = jnp.where((mine >= base) & (mine < base + blocks), mine - base, 0)
    for p in range(tok_size):
        here = (mine >= p * blocks) & (mine < (p + 1) * blocks)
        first = jnp.min(jnp.where(here, mine, tok_size * blocks), axis=1, keepdims=True)
        there = blocks + ((at_tok ^ p) - 1) * 2 + (mine != first).astype(jnp.int32)
        at = jnp.where(here & (p != at_tok), there, at)
    pool_at[...] = at


def routes(place, neighbours, counts, tok_size, blocks):
    usable = jnp.arange(NEIGH)[None, :] < counts[:, None]
    lists = jnp.where(usable, neighbours, -1).reshape(tok_size, blocks * NEIGH)
    vmem = pl.BlockSpec(memory_space=pltpu.VMEM)
    return pl.pallas_call(
        functools.partial(routes_kernel, blocks=blocks),
        out_shape=[
            jax.ShapeDtypeStruct((tok_size, 128), jnp.int32),
            jax.ShapeDtypeStruct((1, blocks * NEIGH), jnp.int32),
        ],
        in_specs=[SMEM, vmem],
        out_specs=[vmem, vmem],
    )(place, lists)


def shards(tokens, qkv_weight, out_weight, neighbours, counts, *, tok_size, hid_size):
    at_tok, at_hid = lax.axis_index("tok"), lax.axis_index("hid")
    blocks = tokens.shape[0] // BLK
    place = jnp.stack([at_hid, at_tok]).astype(jnp.int32)
    heads_here = qkv_weight.shape[1] // (3 * HEAD_WIDTH)
    group = 2 if heads_here % 2 == 0 else 1
    chunks = heads_here // group
    cut = group * HEAD_WIDTH
    far = hid_size - 1
    out_columns = out_weight.shape[1]

    weight = qkv_weight
    near = [s for s in range(2, tok_size) if s & (s - 1) == 0]
    even = range(0, tok_size, 2)
    pieces = [[weight]] + [None] * (tok_size - 1)
    part = line_step((tokens, [], []), "hid", hid_size)
    for s in near:
        pieces[s] = [swap(weight, s, "tok", tok_size)]
    send_ids, pool_at = routes(place, neighbours, counts, tok_size, blocks)
    bits = [1 << i for i in reversed(range(tok_size.bit_length() - 1))]
    out_rows, out_ids = out_weight, [0]
    for bit in bits[:-2]:
        came = swap(out_rows, bit, "tok", tok_size)
        out_rows, out_ids = jnp.concatenate([out_rows, came], axis=0), out_ids + [s ^ bit for s in out_ids]
    came = swap(out_rows, 2, "tok", tok_size)
    for _ in range(far - 1):
        part = line_step(part, "hid", hid_size)
    for s in even:
        if pieces[s] is None:
            pieces[s] = forward(pieces, s, "tok", tok_size)
    for s in even:
        pieces[s + 1] = [swap(x, 1, "tok", tok_size) for x in pieces[s]]
    parts = [part]

    stacks, layout = [], []
    for piece in pieces:
        layout.append([(len(stacks) + i, 0, x.shape[0]) for i, x in enumerate(piece)])
        stacks += piece
    total, last_rows = accumulate(place, parts, stacks, layout, [far - 1], hid_size)
    total, came, send_ids, pool_at = lax.optimization_barrier((total, came, send_ids, pool_at))
    out_rows, out_ids = jnp.concatenate([out_rows, came], axis=0), out_ids + [s ^ 2 for s in out_ids]
    came = swap(out_rows, 1, "tok", tok_size)
    lasts = [(from_left[-1], from_right[-1]) for _, from_left, from_right in parts]
    groups = [
        finish(place, send_ids, total, lasts, last_rows, c * 3 * cut, 3 * cut, hid_size, tok_size // 2)
        for c in range(chunks)
    ]
    parts = []
    for c in range(chunks):
        query, key_values, *sends = groups[c]
        remote = [swap(sends[i], 2 * i, "tok", tok_size) for i in range(1, tok_size // 2)]
        remote, groups[c + 1 :], _ = lax.optimization_barrier(
            (remote, groups[c + 1 :], [p[0] for p in parts])
        )
        passed = jnp.concatenate([sends[0]] + [x[2 * BLK :] for x in remote], axis=0)
        remote = [swap(passed, 1, "tok", tok_size)] + remote
        mixed = attend(place, pool_at, counts, query, key_values, remote, tok_size)
        part = (mixed, [], [])
        for _ in range(far):
            part = line_step(part, "hid", hid_size)
        parts.append(part)
    depth = out_weight.shape[0]
    layout = [[(s not in out_ids, out_ids.index(s if s in out_ids else s ^ 1) * depth, depth)] for s in range(tok_size)]
    layout = [[(int(a), first, n)] for ((a, first, n),) in layout]
    total, last_rows = accumulate(place, parts, [out_rows, came], layout, [far - 1] * chunks, hid_size)
    lasts = [(from_left[-1], from_right[-1]) for _, from_left, from_right in parts]
    (result,) = finish(place, send_ids, total, lasts, last_rows, 0, out_columns, hid_size, 0)
    return result


def solution(mesh):
    placed = (P("tok", "hid"), P("tok", "hid"), P("tok", "hid"), P(), P())
    return jax.shard_map(
        functools.partial(shards, tok_size=mesh.shape["tok"], hid_size=mesh.shape["hid"]),
        mesh=mesh, in_specs=placed, out_specs=P("tok", "hid"), check_vma=False,
    )
```
